256 devices in a mesh: cam: 8 (over x, y_lo), tok: 32 (over z, y_hi, core).
Axes of the slice: x: 4, y: 4 (y_hi: 2, y_lo: 2; y = y_hi * 2 + y_lo), z: 8, core: 2. Of those that a mesh axis runs over, the one named last changes fastest.
Arguments:
- camera_q: bfloat16 [8, 32768, 1536], P('cam', 'tok'), may hold values from -6 to 6
- camera_v: bfloat16 [8, 32768, 1536], P('cam', 'tok'), may hold values from -6 to 6
- lidar_k: bfloat16 [1024, 1536], P('tok'), may hold values from -6 to 6
- lidar_v: bfloat16 [1024, 1536], P('tok'), may hold values from -6 to 6
- head_bias: float32 [12], replicated, may hold values from -2 to 0
Outputs:
- camera_out: bfloat16 [8, 32768, 1536], P('cam', 'tok')
- lidar_out: bfloat16 [1024, 1536], P('tok')
The draws below stay inside these ranges and needn't reach their ends.
All inputs are finite; a program needn't handle non-finite values.
Results may differ from the reference program's by a relative error of at most 0.005.
Values may be sent and summed in bfloat16 or wider, within the bound.
A program may use at most 192 MiB of HBM per device.

```python
import jax
import jax.numpy as jnp
from jax import lax

HEADS = 12
HEAD_DIM = 128
D = 1536
FTOK_DEV = 1024
CAMS = 8
FT = 32768
LTOK = 1024


def level_of(own_key, extent, split, smallest, top_value):
    factor_of, own = 1.0, jax.random.fold_in(own_key, 6)
    for position, shards_of in split:
        steps = jnp.exp(jax.random.uniform(jax.random.fold_in(own, position), (shards_of,), jnp.float32, smallest / len(split), top_value / len(split)))
        factor_of = factor_of * jnp.repeat(steps, extent[position] // shards_of).reshape([-1 if axis == position else 1 for axis in range(len(extent))])
    return factor_of


def noise(key, shape, width, most, cuts=(), kind=jnp.bfloat16):
    drawn = jax.random.normal(key, shape, jnp.float32) * width
    if len(cuts) > 0:
        drawn = level_of(key, shape, cuts, -0.22, 0.18) * drawn
    return jnp.clip(drawn, min=-most, max=most).astype(kind)


def setup_inputs(seed: int = 0) -> dict:
    arg_keys = jax.random.split(jax.random.key(seed), 6)
    return {
        "camera_q": noise(arg_keys[0], (CAMS, FT, D), 1.0, 6.0, ((0, 8), (1, 32))),
        "camera_v": noise(arg_keys[1], (CAMS, FT, D), 1.0, 6.0, ((0, 8), (1, 32))),
        "lidar_k": noise(arg_keys[2], (LTOK, D), 1.0, 6.0, ((0, 32),)),
        "lidar_v": noise(arg_keys[3], (LTOK, D), 1.0, 6.0, ((0, 32),)),
        "head_bias": jnp.clip(jax.random.uniform(arg_keys[4], (HEADS,), jnp.float32, -2.0, 0.0), -2.0, 0.0),
    }


def reference(camera_q, camera_v, lidar_k, lidar_v, head_bias):
    total_rows = CAMS * FT
    blocks = total_rows // FTOK_DEV
    query_blocks = camera_q.reshape(blocks, FTOK_DEV, HEADS, HEAD_DIM)
    value_blocks = camera_v.reshape(blocks, FTOK_DEV, HEADS, HEAD_DIM)
    keys = lidar_k.astype(jnp.float32).reshape(LTOK, HEADS, HEAD_DIM)
    values = lidar_v.astype(jnp.float32).reshape(LTOK, HEADS, HEAD_DIM)
    inverse_root = 1.0 / (HEAD_DIM ** 0.5)

    def one_block(carry, pieces):
        query_block, value_block = pieces
        scores = jnp.einsum("the,lhe->htl", query_block.astype(jnp.float32), keys) * inverse_root
        scores = scores + head_bias[:, None, None]
        weight = jax.nn.sigmoid(scores).astype(jnp.bfloat16)
        weight = lax.optimization_barrier(weight).astype(jnp.float32)
        camera_part = jnp.einsum("htl,lhe->the", weight, values)
        carry = carry + jnp.einsum("htl,the->lhe", weight, value_block.astype(jnp.float32))
        return carry, camera_part

    start = jnp.zeros((LTOK, HEADS, HEAD_DIM), jnp.float32)
    lidar_total, camera_parts = lax.scan(one_block, start, (query_blocks, value_blocks))
    camera_out = (camera_parts.reshape(CAMS, FT, HEADS * HEAD_DIM) / (LTOK ** 0.5)).astype(jnp.bfloat16)
    lidar_out = (lidar_total.reshape(LTOK, HEADS * HEAD_DIM) / ((CAMS * FT) ** 0.5)).astype(jnp.bfloat16)
    return camera_out, lidar_out
```

```python
import functools

import jax
import jax.numpy as jnp
from jax import lax
from jax.experimental import pallas as pl
from jax.experimental.pallas import tpu as pltpu
from jax.sharding import PartitionSpec as P

HEADS = 12
HEAD_DIM = 128
WIDTH = HEADS * HEAD_DIM
SLOTS = 8
OFFSETS = (0, 1, -1, 2, -2, 3, -3, 4)
GROUPS = ((0, 1), (1, 2), (3, 2), (5, 2), (7, 1))
ROWS = 32
XCOLS = 384
F32, BF16 = jnp.float32, jnp.bfloat16


def kernel(
    q_hbm, cv_hbm, k_hbm, v_hbm, bias, co_hbm, lo_hbm,
    q, cv, kb, vb, u_all, co, pb, crecv, psend, precv, zkeep, zsend, zrecv, lob,
    load_sem, k_send, k_recv, ks_send, ks_recv, v_send, v_recv, vs_send, vs_recv,
    c_send, c_recv, p_send, p_recv, z_send, z_recv, l_send, l_recv, out_sem,
):
    cam, tok = lax.axis_index("cam"), lax.axis_index("tok")
    x, y_lo = cam // 2, cam % 2
    z, y_hi, core = tok // 4, (tok // 2) % 2, tok % 2
    y = y_hi * 2 + y_lo

    def device(dx, dy, dz):
        xx, yy, zz = (x + dx + 4) % 4, (y + dy + 4) % 4, (z + dz + 8) % 8
        return (xx * 2 + yy % 2, zz * 4 + (yy // 2) * 2 + core)

    sibling = (cam, z * 4 + y_hi * 2 + (1 - core))
    mirror = (x * 2 + (1 - y_lo), z * 4 + (1 - y_hi) * 2 + core)
    up, down = device(0, 0, 1), device(0, 0, -1)
    in_plane = [(dx, dy) for dx in range(4) for dy in range(4) if dx + dy > 0]

    loads = [
        pltpu.make_async_copy(k_hbm, kb.at[0, y_hi, core], load_sem.at[0]),
        pltpu.make_async_copy(v_hbm, vb.at[0, y_hi, core], load_sem.at[1]),
        pltpu.make_async_copy(q_hbm, q, load_sem.at[2]),
        pltpu.make_async_copy(cv_hbm, cv, load_sem.at[3]),
    ]
    for copy in loads:
        copy.start()

    barrier = pltpu.get_barrier_semaphore()
    partners = [sibling] + [device(dx, dy, 0) for dx, dy in in_plane] + [device(0, 0, dz) for dz in range(1, 8)]
    for partner in partners:
        pl.semaphore_signal(barrier, inc=1, device_id=partner, device_id_type=pl.DeviceIdType.MESH)
    pl.semaphore_wait(barrier, len(partners))

    drains = []

    def send(src, dst, send_sem, recv_sem, to):
        copy = pltpu.make_async_remote_copy(
            src_ref=src, dst_ref=dst, send_sem=send_sem, recv_sem=recv_sem,
            device_id=to, device_id_type=pl.DeviceIdType.MESH,
        )
        copy.start()
        return copy

    def half(p):
        return y_hi if p == 0 else 1 - y_hi

    class Ring:
        def __init__(self, buf, send_sem, recv_sem, s_send, s_recv):
            self.buf, self.send_sem, self.recv_sem = buf, send_sem, recv_sem
            self.s_send, self.s_recv = s_send, s_recv

        def block(self, slot, p):
            return self.buf.at[slot, half(p), core]

        def hop(self, slot, p, to, into):
            copy = send(self.block(slot, p), self.block(into, p), self.send_sem.at[into, p], self.recv_sem.at[into, p], to)
            drains.append(copy)

        def share(self, slot, p):
            block = self.block(slot, p)
            drains.append(send(block, block, self.s_send.at[slot, p], self.s_recv.at[slot, p], sibling))

        def own(self):
            self.share(0, 0)
            block = self.block(0, 0)
            drains.append(send(block, block, self.send_sem.at[0, 0], self.recv_sem.at[0, 1], mirror))
            self.hop(0, 0, down, 1)
            self.hop(0, 0, up, 2)

        def arrive(self, slot, p):
            block = self.block(slot, p)
            pltpu.make_async_copy(block, block, self.recv_sem.at[slot, p]).wait()
            if slot == 0:
                self.hop(0, p, down, 1)
                self.hop(0, p, up, 2)
            elif slot in (1, 3) or (slot == 5 and p == 0):
                self.hop(slot, p, down, slot + 2)
            elif slot in (2, 4) or (slot == 6 and p == 1):
                self.hop(slot, p, up, slot + 2 if slot < 6 else 7)
            self.share(slot, p)

        def shared(self, slot):
            for p in range(2):
                block = self.buf.at[slot, half(p), 1 - core]
                pltpu.make_async_copy(block, block, self.s_recv.at[slot, p]).wait()

    keys = Ring(kb, k_send, k_recv, ks_send, ks_recv)
    values = Ring(vb, v_send, v_recv, vs_send, vs_recv)

    def head(h):
        return pl.ds(pl.multiple_of(h * HEAD_DIM, HEAD_DIM), HEAD_DIM)

    def attend(group, first, count, unroll):
        slot, ns = GROUPS[group]
        rows = ns * 128

        def body(i, carry):
            for j in range(unroll):
                h = first + i * unroll + j
                key = kb[slot : slot + ns, :, :, :, head(h)].reshape(rows, HEAD_DIM)
                s = lax.dot_general(key, q[:, head(h)], (((1,), (1,)), ((), ())), preferred_element_type=F32)
                u = (jnp.tanh(s * (0.5 / HEAD_DIM**0.5) + bias[h] * 0.5) + 1.0).astype(BF16)
                u_all[h, slot * 128 : slot * 128 + rows, :] = u
                part = jnp.dot(u, cv[:, head(h)], preferred_element_type=F32)
                pb[slot : slot + ns, :, :, :, head(h)] = part.astype(BF16).reshape(ns, 2, 2, ROWS, HEAD_DIM)
            return carry

        lax.fori_loop(0, count // unroll, body, 0)

    def core_send(group):
        slot, ns = GROUPS[group]
        src = pb.at[pl.ds(slot, ns), :, 1 - core]
        drains.append(send(src, crecv.at[pl.ds(slot, ns)], c_send.at[group], c_recv.at[group], sibling))

    def plane_send(group):
        slot, ns = GROUPS[group]
        block = crecv.at[pl.ds(slot, ns)]
        pltpu.make_async_copy(block, block, c_recv.at[group]).wait()
        for s in range(slot, slot + ns):
            for hi in range(2):
                total = pb[s, hi, core].astype(F32) + crecv[s, hi].astype(F32)
                psend[s, hi] = total.astype(BF16)
        for dx, dy in in_plane:
            xx, yy = (x + dx) % 4, (y + dy) % 4
            rows = pl.ds(pl.multiple_of((yy % 2) * 16, 16), 16)
            cols = pl.ds(pl.multiple_of(xx * XCOLS, XCOLS), XCOLS)
            src = psend.at[pl.ds(slot, ns), yy // 2, rows, cols]
            send(src, precv.at[dx * 4 + dy, pl.ds(slot, ns)], p_send.at[group], p_recv.at[group], device(dx, dy, 0))

    def plane_sum(group):
        slot, ns = GROUPS[group]
        block = precv.at[pl.ds(1, 15), pl.ds(slot, ns)]
        pltpu.make_async_copy(block, block, p_recv.at[group]).wait()
        rows = pl.ds(pl.multiple_of(y_lo * 16, 16), 16)
        cols = pl.ds(pl.multiple_of(x * XCOLS, XCOLS), XCOLS)
        for s in range(slot, slot + ns):
            total = psend[s, y_hi, rows, cols].astype(F32)
            for i in range(1, 16):
                total = total + precv[i, s].astype(F32)
            if s == 0:
                zkeep[...] = total
            else:
                zsend[s] = total.astype(BF16)
                send(zsend.at[s], zrecv.at[s], z_send, z_recv, device(0, 0, OFFSETS[s]))

    def finish():
        block = zrecv.at[pl.ds(1, 7)]
        pltpu.make_async_copy(block, block, z_recv).wait()
        total = zkeep[...]
        for s in range(1, SLOTS):
            total = total + zrecv[s].astype(F32)
        rows = pl.ds(pl.multiple_of(y_lo * 16, 16), 16)
        cols = pl.ds(pl.multiple_of(x * XCOLS, XCOLS), XCOLS)
        lob[rows, cols] = (total * (1.0 / 1024.0)).astype(BF16)
        mine = lob.at[rows, cols]
        for dx in range(4):
            for dl in range(2):
                if dx + dl > 0:
                    to = (((x + dx) % 4) * 2 + (y_lo + dl) % 2, tok)
                    send(mine, mine, l_send, l_recv, to)

    def camera(first, count, unroll):
        def body(i, carry):
            for j in range(unroll):
                h = first + i * unroll + j
                value = vb[:, :, :, :, head(h)].reshape(SLOTS * 128, HEAD_DIM)
                out = jnp.dot(value.T, u_all[h], preferred_element_type=F32)
                co[:, head(h)] = (out * (1.0 / 64.0)).astype(BF16).T
            cols = pl.ds(pl.multiple_of((first + i * unroll) * HEAD_DIM, HEAD_DIM), unroll * HEAD_DIM)
            pltpu.make_async_copy(co.at[:, cols], co_hbm.at[:, cols], out_sem.at[0]).start()
            return carry

        lax.fori_loop(0, count // unroll, body, 0)

    loads[0].wait()
    keys.own()
    loads[2].wait()
    keys.arrive(0, 1)
    loads[3].wait()
    keys.shared(0)
    attend(0, 0, 6, 3)
    keys.arrive(1, 0)
    keys.arrive(2, 0)
    attend(0, 6, 6, 3)
    core_send(0)
    keys.arrive(1, 1)
    keys.arrive(2, 1)
    keys.shared(1)
    keys.shared(2)
    attend(1, 0, 6, 3)
    plane_send(0)
    keys.arrive(3, 0)
    keys.arrive(4, 0)
    attend(1, 6, 6, 3)
    core_send(1)
    keys.arrive(3, 1)
    keys.arrive(4, 1)
    keys.shared(3)
    keys.shared(4)
    loads[1].wait()
    values.own()
    attend(2, 0, 6, 3)
    plane_send(1)
    plane_sum(0)
    keys.arrive(5, 0)
    keys.arrive(6, 0)
    attend(2, 6, 6, 3)
    core_send(2)
    keys.arrive(5, 1)
    keys.arrive(6, 1)
    keys.shared(5)
    keys.shared(6)
    values.arrive(0, 1)
    attend(3, 0, 6, 3)
    plane_send(2)
    plane_sum(1)
    keys.arrive(7, 0)
    values.arrive(1, 0)
    values.arrive(2, 0)
    attend(3, 6, 6, 3)
    core_send(3)
    keys.arrive(7, 1)
    keys.shared(7)
    values.arrive(1, 1)
    values.arrive(2, 1)
    attend(4, 0, 6, 3)
    plane_send(3)
    plane_sum(2)
    values.arrive(3, 0)
    values.arrive(4, 0)
    attend(4, 6, 6, 3)
    core_send(4)
    values.arrive(3, 1)
    values.arrive(4, 1)
    plane_send(4)
    plane_sum(3)
    values.arrive(5, 0)
    values.arrive(6, 0)
    values.arrive(5, 1)
    values.arrive(6, 1)
    plane_sum(4)
    values.arrive(7, 0)
    values.arrive(7, 1)
    finish()
    for s in range(SLOTS):
        values.shared(s)
    camera(0, 12, 2)

    block = precv.at[pl.ds(0, 7), 0]
    pltpu.make_async_copy(block, block, l_recv).wait()
    out = pltpu.make_async_copy(lob, lo_hbm, out_sem.at[1])
    out.start()
    for copy in drains:
        copy.wait_send()
    for group, (slot, ns) in enumerate(GROUPS):
        block = precv.at[pl.ds(1, 15), pl.ds(slot, ns)]
        pltpu.make_async_copy(block, block, p_send.at[group]).wait()
    block = zsend.at[pl.ds(1, 7)]
    pltpu.make_async_copy(block, block, z_send).wait()
    block = precv.at[pl.ds(0, 7), 0]
    pltpu.make_async_copy(block, block, l_send).wait()
    pltpu.make_async_copy(co, co_hbm, out_sem.at[0]).wait()
    out.wait()


def shards(camera_q, camera_v, lidar_k, lidar_v, head_bias):
    tokens = camera_q.shape[1]
    hbm = pl.BlockSpec(memory_space=pl.ANY)
    dma = pltpu.SemaphoreType.DMA
    planes = (SLOTS, 2, 2, ROWS, WIDTH)
    camera_out, lidar_out = pl.pallas_call(
        kernel,
        out_shape=[
            jax.ShapeDtypeStruct((tokens, WIDTH), BF16),
            jax.ShapeDtypeStruct((ROWS, WIDTH), BF16),
        ],
        in_specs=[hbm, hbm, hbm, hbm, pl.BlockSpec(memory_space=pltpu.SMEM)],
        out_specs=[hbm, hbm],
        scratch_shapes=[
            pltpu.VMEM((tokens, WIDTH), BF16),
            pltpu.VMEM((tokens, WIDTH), BF16),
            pltpu.VMEM(planes, BF16),
            pltpu.VMEM(planes, BF16),
            pltpu.VMEM((HEADS, SLOTS * 128, tokens), BF16),
            pltpu.VMEM((tokens, WIDTH), BF16),
            pltpu.VMEM(planes, BF16),
            pltpu.VMEM((SLOTS, 2, ROWS, WIDTH), BF16),
            pltpu.VMEM((SLOTS, 2, ROWS, WIDTH), BF16),
            pltpu.VMEM((16, SLOTS, 16, XCOLS), BF16),
            pltpu.VMEM((16, XCOLS), F32),
            pltpu.VMEM((SLOTS, 16, XCOLS), BF16),
            pltpu.VMEM((SLOTS, 16, XCOLS), BF16),
            pltpu.VMEM((ROWS, WIDTH), BF16),
            dma((4,)),
            dma((SLOTS, 2)), dma((SLOTS, 2)), dma((SLOTS, 2)), dma((SLOTS, 2)),
            dma((SLOTS, 2)), dma((SLOTS, 2)), dma((SLOTS, 2)), dma((SLOTS, 2)),
            dma((5,)), dma((5,)), dma((5,)), dma((5,)),
            dma, dma, dma, dma,
            dma((2,)),
        ],
        compiler_params=pltpu.CompilerParams(
            collective_id=0, has_side_effects=True, vmem_limit_bytes=60 << 20
        ),
        name="fused",
    )(camera_q.reshape(tokens, WIDTH), camera_v.reshape(tokens, WIDTH), lidar_k, lidar_v, head_bias)
    return camera_out.reshape(camera_q.shape), lidar_out


def solution(mesh):
    return jax.shard_map(
        shards,
        mesh=mesh,
        in_specs=(
            P("cam", "tok", None),
            P("cam", "tok", None),
            P("tok", None),
            P("tok", None),
            P(),
        ),
        out_specs=(P("cam", "tok", None), P("tok", None)),
        check_vma=False,
    )
```

```python
import functools

import jax
import jax.numpy as jnp
from jax import lax
from jax.experimental import pallas as pl
from jax.experimental.pallas import tpu as pltpu
from jax.sharding import PartitionSpec as P

HEADS = 12
HEAD_DIM = 128
WIDTH = HEADS * HEAD_DIM
SLOTS = 8
OFFSETS = (0, 1, -1, 2, -2, 3, -3, 4)
GROUPS = ((0, 1), (1, 2), (3, 2), (5, 2), (7, 1))
ROWS = 32
XCOLS = 384
F32, BF16 = jnp.float32, jnp.bfloat16


def kernel(
    q_hbm, cv_hbm, k_hbm, v_hbm, bias, co, lo,
    q, cv, kb, vb, u_all, pb, crecv, psend, precv, zkeep, zsend, zrecv, lob,
    load_sem, k_send, k_recv, ks_send, ks_recv, v_send, v_recv, vs_send, vs_recv,
    c_send, c_recv, p_send, p_recv, z_send, z_recv, l_send, l_recv,
):
    cam, tok = lax.axis_index("cam"), lax.axis_index("tok")
    x, y_lo = cam // 2, cam % 2
    z, y_hi, core = tok // 4, (tok // 2) % 2, tok % 2
    y = y_hi * 2 + y_lo

    def device(dx, dy, dz):
        xx, yy, zz = (x + dx + 4) % 4, (y + dy + 4) % 4, (z + dz + 8) % 8
        return (xx * 2 + yy % 2, zz * 4 + (yy // 2) * 2 + core)

    sibling = (cam, z * 4 + y_hi * 2 + (1 - core))
    mirror = (x * 2 + (1 - y_lo), z * 4 + (1 - y_hi) * 2 + core)
    up, down = device(0, 0, 1), device(0, 0, -1)
    in_plane = [(dx, dy) for dx in range(4) for dy in range(4) if dx + dy > 0]

    loads = [
        pltpu.make_async_copy(k_hbm, kb.at[0, y_hi, core], load_sem.at[0]),
        pltpu.make_async_copy(v_hbm, vb.at[0, y_hi, core], load_sem.at[1]),
        pltpu.make_async_copy(q_hbm, q, load_sem.at[2]),
        pltpu.make_async_copy(cv_hbm, cv, load_sem.at[3]),
    ]
    for copy in loads:
        copy.start()

    barrier = pltpu.get_barrier_semaphore()
    partners = [sibling] + [device(dx, dy, 0) for dx, dy in in_plane] + [device(0, 0, dz) for dz in range(1, 8)]
    for partner in partners:
        pl.semaphore_signal(barrier, inc=1, device_id=partner, device_id_type=pl.DeviceIdType.MESH)
    pl.semaphore_wait(barrier, len(partners))

    drains = []

    def send(src, dst, send_sem, recv_sem, to):
        copy = pltpu.make_async_remote_copy(
            src_ref=src, dst_ref=dst, send_sem=send_sem, recv_sem=recv_sem,
            device_id=to, device_id_type=pl.DeviceIdType.MESH,
        )
        copy.start()
        return copy

    def half(p):
        return y_hi if p == 0 else 1 - y_hi

    class Ring:
        def __init__(self, buf, send_sem, recv_sem, s_send, s_recv):
            self.buf, self.send_sem, self.recv_sem = buf, send_sem, recv_sem
            self.s_send, self.s_recv = s_send, s_recv

        def block(self, slot, p):
            return self.buf.at[slot, half(p), core]

        def hop(self, slot, p, to, into):
            copy = send(self.block(slot, p), self.block(into, p), self.send_sem.at[into, p], self.recv_sem.at[into, p], to)
            drains.append(copy)

        def share(self, slot, p):
            block = self.block(slot, p)
            drains.append(send(block, block, self.s_send.at[slot, p], self.s_recv.at[slot, p], sibling))

        def near(self):
            block = self.block(0, 0)
            drains.append(send(block, block, self.send_sem.at[0, 0], self.recv_sem.at[0, 1], mirror))
            self.share(0, 0)

        def begin(self, p):
            self.hop(0, p, down, 1)
            self.hop(0, p, up, 2)

        def arrive(self, slot, p):
            block = self.block(slot, p)
            pltpu.make_async_copy(block, block, self.recv_sem.at[slot, p]).wait()
            if slot == 0:
                self.begin(p)
            elif slot in (1, 3) or (slot == 5 and p == 0):
                self.hop(slot, p, down, slot + 2)
            elif slot in (2, 4) or (slot == 6 and p == 1):
                self.hop(slot, p, up, slot + 2 if slot < 6 else 7)
            self.share(slot, p)

        def shared(self, slot):
            for p in range(2):
                block = self.buf.at[slot, half(p), 1 - core]
                pltpu.make_async_copy(block, block, self.s_recv.at[slot, p]).wait()

    keys = Ring(kb, k_send, k_recv, ks_send, ks_recv)
    values = Ring(vb, v_send, v_recv, vs_send, vs_recv)

    def head(h):
        return pl.ds(h * HEAD_DIM if isinstance(h, int) else pl.multiple_of(h * HEAD_DIM, HEAD_DIM), HEAD_DIM)

    def attend(group, first, count):
        slot, ns = GROUPS[group]
        rows = ns * 128

        for h in range(first, first + count):
            key = kb[slot : slot + ns, :, :, :, head(h)].reshape(rows, HEAD_DIM)
            s = lax.dot_general(key, q[:, head(h)], (((1,), (1,)), ((), ())), preferred_element_type=F32)
            u = (jnp.tanh(s * (0.5 / HEAD_DIM**0.5) + bias[h] * 0.5) + 1.0).astype(BF16)
            u_all[h, slot * 128 : slot * 128 + rows, :] = u
            part = jnp.dot(u, cv[:, head(h)], preferred_element_type=F32)
            pb[slot : slot + ns, :, :, :, head(h)] = part.astype(BF16).reshape(ns, 2, 2, ROWS, HEAD_DIM)

    def core_send(group):
        slot, ns = GROUPS[group]
        src = pb.at[pl.ds(slot, ns), :, 1 - core]
        drains.append(send(src, crecv.at[pl.ds(slot, ns)], c_send.at[group], c_recv.at[group], sibling))

    def plane_send(group):
        slot, ns = GROUPS[group]
        block = crecv.at[pl.ds(slot, ns)]
        pltpu.make_async_copy(block, block, c_recv.at[group]).wait()
        for s in range(slot, slot + ns):
            for hi in range(2):
                total = pb[s, hi, core].astype(F32) + crecv[s, hi].astype(F32)
                psend[s, hi] = total.astype(BF16)
        for dx, dy in in_plane:
            xx, yy = (x + dx) % 4, (y + dy) % 4
            rows = pl.ds(pl.multiple_of((yy % 2) * 16, 16), 16)
            cols = pl.ds(pl.multiple_of(xx * XCOLS, XCOLS), XCOLS)
            src = psend.at[pl.ds(slot, ns), yy // 2, rows, cols]
            send(src, precv.at[dx * 4 + dy, pl.ds(slot, ns)], p_send.at[group], p_recv.at[group], device(dx, dy, 0))

    def plane_sum(group):
        slot, ns = GROUPS[group]
        block = precv.at[pl.ds(1, 15), pl.ds(slot, ns)]
        pltpu.make_async_copy(block, block, p_recv.at[group]).wait()
        rows = pl.ds(pl.multiple_of(y_lo * 16, 16), 16)
        cols = pl.ds(pl.multiple_of(x * XCOLS, XCOLS), XCOLS)
        for s in range(slot, slot + ns):
            total = psend[s, y_hi, rows, cols].astype(F32)
            for i in range(1, 16):
                total = total + precv[i, s].astype(F32)
            if s == 0:
                zkeep[...] = total
            else:
                zsend[s] = total.astype(BF16)
                send(zsend.at[s], zrecv.at[s], z_send, z_recv, device(0, 0, OFFSETS[s]))

    def finish():
        block = zrecv.at[pl.ds(1, 7)]
        pltpu.make_async_copy(block, block, z_recv).wait()
        total = zkeep[...]
        for s in range(1, SLOTS):
            total = total + zrecv[s].astype(F32)
        rows = pl.ds(pl.multiple_of(y_lo * 16, 16), 16)
        cols = pl.ds(pl.multiple_of(x * XCOLS, XCOLS), XCOLS)
        lob[rows, cols] = (total * (1.0 / 1024.0)).astype(BF16)
        mine = lob.at[rows, cols]
        for dx in range(4):
            for dl in range(2):
                if dx + dl > 0:
                    to = (((x + dx) % 4) * 2 + (y_lo + dl) % 2, tok)
                    send(mine, mine, l_send, l_recv, to)

    def camera(first, count, unroll):
        def body(i, carry):
            for j in range(unroll):
                h = first + i * unroll + j
                value = vb[:, :, :, :, head(h)].reshape(SLOTS * 128, HEAD_DIM)
                out = jnp.dot(value.T, u_all[h], preferred_element_type=F32)
                co[:, head(h)] = (out * (1.0 / 64.0)).astype(BF16).T
            return carry

        lax.fori_loop(0, count // unroll, body, 0)

    loads[0].wait()
    keys.near()
    keys.begin(0)
    loads[1].wait()
    values.near()
    keys.arrive(0, 1)
    keys.arrive(1, 0)
    keys.arrive(2, 0)
    loads[2].wait()
    loads[3].wait()
    keys.shared(0)
    attend(0, 0, 6)
    keys.arrive(1, 1)
    keys.arrive(2, 1)
    attend(0, 6, 6)
    core_send(0)
    keys.arrive(3, 0)
    keys.arrive(4, 0)
    keys.shared(1)
    keys.shared(2)
    attend(1, 0, 6)
    keys.arrive(3, 1)
    keys.arrive(4, 1)
    values.begin(0)
    values.arrive(0, 1)
    plane_send(0)
    attend(1, 6, 6)
    core_send(1)
    keys.arrive(5, 0)
    keys.arrive(6, 0)
    keys.shared(3)
    keys.shared(4)
    attend(2, 0, 6)
    keys.arrive(5, 1)
    keys.arrive(6, 1)
    plane_send(1)
    attend(2, 6, 6)
    core_send(2)
    plane_sum(0)
    keys.arrive(7, 0)
    keys.shared(5)
    keys.shared(6)
    attend(3, 0, 6)
    keys.arrive(7, 1)
    values.arrive(1, 0)
    values.arrive(2, 0)
    plane_send(2)
    attend(3, 6, 6)
    core_send(3)
    plane_sum(1)
    values.arrive(1, 1)
    values.arrive(2, 1)
    keys.shared(7)
    attend(4, 0, 6)
    plane_send(3)
    values.arrive(3, 0)
    values.arrive(4, 0)
    attend(4, 6, 6)
    core_send(4)
    plane_sum(2)
    values.arrive(3, 1)
    values.arrive(4, 1)
    plane_send(4)
    plane_sum(3)
    values.arrive(5, 0)
    values.arrive(6, 0)
    values.arrive(5, 1)
    values.arrive(6, 1)
    plane_sum(4)
    values.arrive(7, 0)
    values.arrive(7, 1)
    for s in range(SLOTS):
        values.shared(s)
    camera(0, 6, 2)
    finish()
    camera(6, 6, 2)

    block = precv.at[pl.ds(0, 7), 0]
    pltpu.make_async_copy(block, block, l_recv).wait()
    lo[...] = lob[...]
    for copy in drains:
        copy.wait_send()
    for group, (slot, ns) in enumerate(GROUPS):
        block = precv.at[pl.ds(1, 15), pl.ds(slot, ns)]
        pltpu.make_async_copy(block, block, p_send.at[group]).wait()
    block = zsend.at[pl.ds(1, 7)]
    pltpu.make_async_copy(block, block, z_send).wait()
    block = precv.at[pl.ds(0, 7), 0]
    pltpu.make_async_copy(block, block, l_send).wait()


def shards(camera_q, camera_v, lidar_k, lidar_v, head_bias):
    tokens = camera_q.shape[1]
    hbm = pl.BlockSpec(memory_space=pl.ANY)
    dma = pltpu.SemaphoreType.DMA
    planes = (SLOTS, 2, 2, ROWS, WIDTH)
    camera_out, lidar_out = pl.pallas_call(
        kernel,
        out_shape=[
            pltpu.VMEM((tokens, WIDTH), BF16),
            pltpu.VMEM((ROWS, WIDTH), BF16),
        ],
        in_specs=[hbm, hbm, hbm, hbm, pl.BlockSpec(memory_space=pltpu.SMEM)],
        out_specs=[pl.BlockSpec(memory_space=pltpu.VMEM)] * 2,
        scratch_shapes=[
            pltpu.VMEM((tokens, WIDTH), BF16),
            pltpu.VMEM((tokens, WIDTH), BF16),
            pltpu.VMEM(planes, BF16),
            pltpu.VMEM(planes, BF16),
            pltpu.VMEM((HEADS, SLOTS * 128, tokens), BF16),
            pltpu.VMEM(planes, BF16),
            pltpu.VMEM((SLOTS, 2, ROWS, WIDTH), BF16),
            pltpu.VMEM((SLOTS, 2, ROWS, WIDTH), BF16),
            pltpu.VMEM((16, SLOTS, 16, XCOLS), BF16),
            pltpu.VMEM((16, XCOLS), F32),
            pltpu.VMEM((SLOTS, 16, XCOLS), BF16),
            pltpu.VMEM((SLOTS, 16, XCOLS), BF16),
            pltpu.VMEM((ROWS, WIDTH), BF16),
            dma((4,)),
            dma((SLOTS, 2)), dma((SLOTS, 2)), dma((SLOTS, 2)), dma((SLOTS, 2)),
            dma((SLOTS, 2)), dma((SLOTS, 2)), dma((SLOTS, 2)), dma((SLOTS, 2)),
            dma((5,)), dma((5,)), dma((5,)), dma((5,)),
            dma, dma, dma, dma,
        ],
        compiler_params=pltpu.CompilerParams(
            collective_id=0, has_side_effects=True, vmem_limit_bytes=54 << 20
        ),
        name="fused",
    )(camera_q.reshape(tokens, WIDTH), camera_v.reshape(tokens, WIDTH), lidar_k, lidar_v, head_bias)
    return camera_out.reshape(camera_q.shape), lidar_out


def solution(mesh):
    return jax.shard_map(
        shards,
        mesh=mesh,
        in_specs=(
            P("cam", "tok", None),
            P("cam", "tok", None),
            P("tok", None),
            P("tok", None),
            P(),
        ),
        out_specs=(P("cam", "tok", None), P("tok", None)),
        check_vma=False,
    )
```

```python
import functools

import jax
import jax.numpy as jnp
from jax import lax
from jax.experimental import pallas as pl
from jax.experimental.pallas import tpu as pltpu
from jax.sharding import PartitionSpec as P

HEADS = 12
HEAD_DIM = 128
WIDTH = HEADS * HEAD_DIM
SLOTS = 8
OFFSETS = (0, 1, -1, 2, -2, 3, -3, 4)
GROUPS = ((0, 1), (1, 2), (3, 2), (5, 2), (7, 1))
ROWS = 32
XCOLS = 384
HALF = WIDTH // 2
F32, BF16 = jnp.float32, jnp.bfloat16


def kernel(
    q_hbm, cv_hbm, k_hbm, v_hbm, bias, co, lo,
    q, cv, kb, vb, u_all, pb, crecv, psend, precv, zkeep, zsend, zrecv, lob,
    load_sem, k_send, k_recv, ks_send, ks_recv, n_send, n_recv, v_send, v_recv, vx_send, vx_recv, vs_send, vs_recv,
    c_send, c_recv, p_send, p_recv, z_send, z_recv, l_send, l_recv,
):
    cam, tok = lax.axis_index("cam"), lax.axis_index("tok")
    x, y_lo = cam // 2, cam % 2
    z, y_hi, core = tok // 4, (tok // 2) % 2, tok % 2
    y = y_hi * 2 + y_lo

    def device(dx, dy, dz):
        xx, yy, zz = (x + dx + 4) % 4, (y + dy + 4) % 4, (z + dz + 8) % 8
        return (xx * 2 + yy % 2, zz * 4 + (yy // 2) * 2 + core)

    sibling = (cam, z * 4 + y_hi * 2 + (1 - core))
    mirror = (x * 2 + (1 - y_lo), z * 4 + (1 - y_hi) * 2 + core)
    up, down = device(0, 0, 1), device(0, 0, -1)
    right, left = device(1, 0, 0), device(-1, 0, 0)
    in_plane = [(dx, dy) for dx in range(4) for dy in range(4) if dx + dy > 0]

    loads = [
        pltpu.make_async_copy(k_hbm, kb.at[0, y_hi, core], load_sem.at[0]),
        pltpu.make_async_copy(v_hbm, vb.at[0, y_hi, core], load_sem.at[1]),
        pltpu.make_async_copy(q_hbm, q, load_sem.at[2]),
        pltpu.make_async_copy(cv_hbm, cv, load_sem.at[3]),
    ]
    for copy in loads:
        copy.start()

    barrier = pltpu.get_barrier_semaphore()
    partners = [sibling] + [device(dx, dy, 0) for dx, dy in in_plane] + [device(0, 0, dz) for dz in range(1, 8)]
    for partner in partners:
        pl.semaphore_signal(barrier, inc=1, device_id=partner, device_id_type=pl.DeviceIdType.MESH)
    pl.semaphore_wait(barrier, len(partners))

    drains = []

    def send(src, dst, send_sem, recv_sem, to):
        copy = pltpu.make_async_remote_copy(
            src_ref=src, dst_ref=dst, send_sem=send_sem, recv_sem=recv_sem,
            device_id=to, device_id_type=pl.DeviceIdType.MESH,
        )
        copy.start()
        return copy

    def half(p):
        return y_hi if p == 0 else 1 - y_hi

    class Ring:
        def __init__(self, buf, send_sem, recv_sem, s_send, s_recv):
            self.buf, self.send_sem, self.recv_sem = buf, send_sem, recv_sem
            self.s_send, self.s_recv = s_send, s_recv

        def block(self, slot, p):
            return self.buf.at[slot, half(p), core]

        def hop(self, slot, p, to, into):
            copy = send(self.block(slot, p), self.block(into, p), self.send_sem.at[into, p], self.recv_sem.at[into, p], to)
            drains.append(copy)

        def share(self, slot, p):
            block = self.block(slot, p)
            drains.append(send(block, block, self.s_send.at[slot, p], self.s_recv.at[slot, p], sibling))

        def near(self):
            block = self.block(0, 0)
            drains.append(send(block, block, self.send_sem.at[0, 0], self.recv_sem.at[0, 1], mirror))
            self.share(0, 0)

        def begin(self, p):
            self.hop(0, p, down, 1)
            self.hop(0, p, up, 2)

        def arrive(self, slot, p):
            block = self.block(slot, p)
            pltpu.make_async_copy(block, block, self.recv_sem.at[slot, p]).wait()
            if slot == 0:
                self.begin(p)
            elif slot in (1, 3) or (slot == 5 and p == 0):
                self.hop(slot, p, down, slot + 2)
            elif slot in (2, 4) or (slot == 6 and p == 1):
                self.hop(slot, p, up, slot + 2 if slot < 6 else 7)
            self.share(slot, p)

        def shared(self, slot):
            for p in range(2):
                block = self.buf.at[slot, half(p), 1 - core]
                pltpu.make_async_copy(block, block, self.s_recv.at[slot, p]).wait()

    class HalfRing:
        def __init__(self, buf, near_send, near_recv, send_sem, recv_sem, x_send, x_recv, s_send, s_recv):
            self.buf, self.near_send, self.near_recv = buf, near_send, near_recv
            self.send_sem, self.recv_sem, self.x_send, self.x_recv = send_sem, recv_sem, x_send, x_recv
            self.s_send, self.s_recv = s_send, s_recv

        def block(self, slot, p, side, which=None):
            cols = pl.ds(pl.multiple_of((x + side) % 2 * HALF, HALF), HALF)
            return self.buf.at[slot, half(p), core if which is None else which, :, cols]

        def near(self):
            block = self.buf.at[0, y_hi, core]
            drains.append(send(block, block, self.near_send.at[0], self.near_recv.at[0], mirror))
            drains.append(send(block, block, self.near_send.at[1], self.near_recv.at[1], sibling))

        def near_arrive(self):
            block = self.buf.at[0, 1 - y_hi, core]
            pltpu.make_async_copy(block, block, self.near_recv.at[0]).wait()
            drains.append(send(block, block, self.near_send.at[2], self.near_recv.at[2], sibling))

        def hop(self, slot, p, to, into):
            copy = send(self.block(slot, p, 0), self.block(into, p, 0), self.send_sem.at[into, p], self.recv_sem.at[into, p], to)
            drains.append(copy)

        def begin(self):
            for p in range(2):
                self.hop(0, p, down, 1)
                self.hop(0, p, up, 2)

        def share(self, slot, p, side):
            block = self.block(slot, p, side)
            drains.append(send(block, block, self.s_send.at[side, slot, p], self.s_recv.at[side, slot, p], sibling))

        def arrive(self, slot, p):
            block = self.block(slot, p, 0)
            pltpu.make_async_copy(block, block, self.recv_sem.at[slot, p]).wait()
            if slot in (1, 3) or (slot == 5 and p == 0):
                self.hop(slot, p, down, slot + 2)
            elif slot in (2, 4) or (slot == 6 and p == 1):
                self.hop(slot, p, up, slot + 2 if slot < 6 else 7)
            to = right if p == 0 else left
            drains.append(send(block, block, self.x_send.at[slot, p], self.x_recv.at[slot, p], to))
            self.share(slot, p, 0)

        def cross(self, slot):
            for p in range(2):
                block = self.block(slot, p, 1)
                pltpu.make_async_copy(block, block, self.x_recv.at[slot, p]).wait()
                self.share(slot, p, 1)

        def shared(self):
            for i in range(2):
                block = self.buf.at[0, half(i), 1 - core]
                pltpu.make_async_copy(block, block, self.near_recv.at[1 + i]).wait()
            for slot in range(1, SLOTS):
                for p in range(2):
                    for side in range(2):
                        block = self.block(slot, p, side, 1 - core)
                        pltpu.make_async_copy(block, block, self.s_recv.at[side, slot, p]).wait()

    keys = Ring(kb, k_send, k_recv, ks_send, ks_recv)
    values = HalfRing(vb, n_send, n_recv, v_send, v_recv, vx_send, vx_recv, vs_send, vs_recv)

    def head(h):
        return pl.ds(h * HEAD_DIM if isinstance(h, int) else pl.multiple_of(h * HEAD_DIM, HEAD_DIM), HEAD_DIM)

    def attend(group, first, count):
        slot, ns = GROUPS[group]
        rows = ns * 128

        for h in range(first, first + count):
            key = kb[slot : slot + ns, :, :, :, head(h)].reshape(rows, HEAD_DIM)
            s = lax.dot_general(key, q[:, head(h)], (((1,), (1,)), ((), ())), preferred_element_type=F32)
            u = (jnp.tanh(s * (0.5 / HEAD_DIM**0.5) + bias[h] * 0.5) + 1.0).astype(BF16)
            u_all[h, slot * 128 : slot * 128 + rows, :] = u
            part = jnp.dot(u, cv[:, head(h)], preferred_element_type=F32)
            pb[slot : slot + ns, :, :, :, head(h)] = part.astype(BF16).reshape(ns, 2, 2, ROWS, HEAD_DIM)

    def core_send(group):
        slot, ns = GROUPS[group]
        src = pb.at[pl.ds(slot, ns), :, 1 - core]
        drains.append(send(src, crecv.at[pl.ds(slot, ns)], c_send.at[group], c_recv.at[group], sibling))

    def plane_send(group):
        slot, ns = GROUPS[group]
        block = crecv.at[pl.ds(slot, ns)]
        pltpu.make_async_copy(block, block, c_recv.at[group]).wait()
        for s in range(slot, slot + ns):
            for hi in range(2):
                total = pb[s, hi, core].astype(F32) + crecv[s, hi].astype(F32)
                psend[s, hi] = total.astype(BF16)
        for dx, dy in in_plane:
            xx, yy = (x + dx) % 4, (y + dy) % 4
            rows = pl.ds(pl.multiple_of((yy % 2) * 16, 16), 16)
            cols = pl.ds(pl.multiple_of(xx * XCOLS, XCOLS), XCOLS)
            src = psend.at[pl.ds(slot, ns), yy // 2, rows, cols]
            send(src, precv.at[dx * 4 + dy, pl.ds(slot, ns)], p_send.at[group], p_recv.at[group], device(dx, dy, 0))

    def plane_sum(group):
        slot, ns = GROUPS[group]
        block = precv.at[pl.ds(1, 15), pl.ds(slot, ns)]
        pltpu.make_async_copy(block, block, p_recv.at[group]).wait()
        rows = pl.ds(pl.multiple_of(y_lo * 16, 16), 16)
        cols = pl.ds(pl.multiple_of(x * XCOLS, XCOLS), XCOLS)
        for s in range(slot, slot + ns):
            total = psend[s, y_hi, rows, cols].astype(F32)
            for i in range(1, 16):
                total = total + precv[i, s].astype(F32)
            if s == 0:
                zkeep[...] = total
            else:
                zsend[s] = total.astype(BF16)
                send(zsend.at[s], zrecv.at[s], z_send, z_recv, device(0, 0, OFFSETS[s]))

    def finish():
        block = zrecv.at[pl.ds(1, 7)]
        pltpu.make_async_copy(block, block, z_recv).wait()
        total = zkeep[...]
        for s in range(1, SLOTS):
            total = total + zrecv[s].astype(F32)
        rows = pl.ds(pl.multiple_of(y_lo * 16, 16), 16)
        cols = pl.ds(pl.multiple_of(x * XCOLS, XCOLS), XCOLS)
        lob[rows, cols] = (total * (1.0 / 1024.0)).astype(BF16)
        mine = lob.at[rows, cols]
        for dx in range(4):
            for dl in range(2):
                if dx + dl > 0:
                    to = (((x + dx) % 4) * 2 + (y_lo + dl) % 2, tok)
                    send(mine, mine, l_send, l_recv, to)

    def camera(first, count, unroll):
        def body(i, carry):
            for j in range(unroll):
                h = first + i * unroll + j
                value = vb[:, :, :, :, head(h)].reshape(SLOTS * 128, HEAD_DIM)
                out = jnp.dot(value.T, u_all[h], preferred_element_type=F32)
                co[:, head(h)] = (out * (1.0 / 64.0)).astype(BF16).T
            return carry

        lax.fori_loop(0, count // unroll, body, 0)

    loads[0].wait()
    keys.near()
    keys.begin(0)
    loads[1].wait()
    values.near()
    keys.arrive(0, 1)
    keys.arrive(1, 0)
    keys.arrive(2, 0)
    loads[2].wait()
    loads[3].wait()
    keys.shared(0)
    attend(0, 0, 6)
    keys.arrive(1, 1)
    keys.arrive(2, 1)
    values.near_arrive()
    attend(0, 6, 6)
    core_send(0)
    keys.arrive(3, 0)
    keys.arrive(4, 0)
    values.begin()
    keys.shared(1)
    keys.shared(2)
    attend(1, 0, 6)
    keys.arrive(3, 1)
    keys.arrive(4, 1)
    values.arrive(1, 0)
    values.arrive(2, 0)
    plane_send(0)
    attend(1, 6, 6)
    core_send(1)
    keys.arrive(5, 0)
    keys.arrive(6, 0)
    values.arrive(1, 1)
    values.arrive(2, 1)
    keys.shared(3)
    keys.shared(4)
    attend(2, 0, 6)
    keys.arrive(5, 1)
    keys.arrive(6, 1)
    values.arrive(3, 0)
    values.arrive(4, 0)
    plane_send(1)
    attend(2, 6, 6)
    core_send(2)
    keys.arrive(7, 0)
    values.arrive(3, 1)
    values.arrive(4, 1)
    plane_sum(0)
    keys.shared(5)
    keys.shared(6)
    attend(3, 0, 6)
    keys.arrive(7, 1)
    values.arrive(5, 0)
    values.arrive(6, 0)
    plane_send(2)
    attend(3, 6, 6)
    core_send(3)
    values.arrive(5, 1)
    values.arrive(6, 1)
    plane_sum(1)
    values.cross(1)
    values.cross(2)
    keys.shared(7)
    attend(4, 0, 6)
    plane_send(3)
    values.cross(3)
    values.cross(4)
    attend(4, 6, 6)
    core_send(4)
    values.arrive(7, 0)
    plane_sum(2)
    plane_send(4)
    values.arrive(7, 1)
    values.cross(5)
    values.cross(6)
    values.cross(7)
    values.shared()
    camera(0, 6, 2)
    plane_sum(3)
    plane_sum(4)
    camera(6, 6, 2)
    finish()

    block = precv.at[pl.ds(0, 7), 0]
    pltpu.make_async_copy(block, block, l_recv).wait()
    lo[...] = lob[...]
    for copy in drains:
        copy.wait_send()
    for group, (slot, ns) in enumerate(GROUPS):
        block = precv.at[pl.ds(1, 15), pl.ds(slot, ns)]
        pltpu.make_async_copy(block, block, p_send.at[group]).wait()
    block = zsend.at[pl.ds(1, 7)]
    pltpu.make_async_copy(block, block, z_send).wait()
    block = precv.at[pl.ds(0, 7), 0]
    pltpu.make_async_copy(block, block, l_send).wait()


def shards(camera_q, camera_v, lidar_k, lidar_v, head_bias):
    tokens = camera_q.shape[1]
    hbm = pl.BlockSpec(memory_space=pl.ANY)
    dma = pltpu.SemaphoreType.DMA
    planes = (SLOTS, 2, 2, ROWS, WIDTH)
    camera_out, lidar_out = pl.pallas_call(
        kernel,
        out_shape=[
            pltpu.VMEM((tokens, WIDTH), BF16),
            pltpu.VMEM((ROWS, WIDTH), BF16),
        ],
        in_specs=[hbm, hbm, hbm, hbm, pl.BlockSpec(memory_space=pltpu.SMEM)],
        out_specs=[pl.BlockSpec(memory_space=pltpu.VMEM)] * 2,
        scratch_shapes=[
            pltpu.VMEM((tokens, WIDTH), BF16),
            pltpu.VMEM((tokens, WIDTH), BF16),
            pltpu.VMEM(planes, BF16),
            pltpu.VMEM(planes, BF16),
            pltpu.VMEM((HEADS, SLOTS * 128, tokens), BF16),
            pltpu.VMEM(planes, BF16),
            pltpu.VMEM((SLOTS, 2, ROWS, WIDTH), BF16),
            pltpu.VMEM((SLOTS, 2, ROWS, WIDTH), BF16),
            pltpu.VMEM((16, SLOTS, 16, XCOLS), BF16),
            pltpu.VMEM((16, XCOLS), F32),
            pltpu.VMEM((SLOTS, 16, XCOLS), BF16),
            pltpu.VMEM((SLOTS, 16, XCOLS), BF16),
            pltpu.VMEM((ROWS, WIDTH), BF16),
            dma((4,)),
            dma((SLOTS, 2)), dma((SLOTS, 2)), dma((SLOTS, 2)), dma((SLOTS, 2)),
            dma((3,)), dma((3,)),
            dma((SLOTS, 2)), dma((SLOTS, 2)), dma((SLOTS, 2)), dma((SLOTS, 2)),
            dma((2, SLOTS, 2)), dma((2, SLOTS, 2)),
            dma((5,)), dma((5,)), dma((5,)), dma((5,)),
            dma, dma, dma, dma,
        ],
        compiler_params=pltpu.CompilerParams(
            collective_id=0, has_side_effects=True, vmem_limit_bytes=54 << 20
        ),
        name="fused",
    )(camera_q.reshape(tokens, WIDTH), camera_v.reshape(tokens, WIDTH), lidar_k, lidar_v, head_bias)
    return camera_out.reshape(camera_q.shape), lidar_out


def solution(mesh):
    return jax.shard_map(
        shards,
        mesh=mesh,
        in_specs=(
            P("cam", "tok", None),
            P("cam", "tok", None),
            P("tok", None),
            P("tok", None),
            P(),
        ),
        out_specs=(P("cam", "tok", None), P("tok", None)),
        check_vma=False,
    )
```

```python
import functools

import jax
import jax.numpy as jnp
from jax import lax
from jax.experimental import pallas as pl
from jax.experimental.pallas import tpu as pltpu
from jax.sharding import PartitionSpec as P

HEADS = 12
HEAD_DIM = 128
WIDTH = HEADS * HEAD_DIM
SLOTS = 8
OFFSETS = (0, 1, -1, 2, -2, 3, -3, 4)
GROUPS = ((0, 1), (1, 2), (3, 2), (5, 2), (7, 1))
ROWS = 32
XCOLS = 384
F32, BF16 = jnp.float32, jnp.bfloat16


def kernel(
    q_hbm, cv_hbm, k_hbm, v_hbm, bias, co, lo,
    q, cv, kb, vb, u_all, pb, crecv, psend, precv, zkeep, zsend, zrecv, lob,
    load_sem, k_send, k_recv, ks_send, ks_recv, v_send, v_recv,
    c_send, c_recv, p_send, p_recv, z_send, z_recv, l_send, l_recv,
):
    cam, tok = lax.axis_index("cam"), lax.axis_index("tok")
    x, y_lo = cam // 2, cam % 2
    z, y_hi, core = tok // 4, (tok // 2) % 2, tok % 2
    y = y_hi * 2 + y_lo

    def device(dx, dy, dz):
        xx, yy, zz = (x + dx + 4) % 4, (y + dy + 4) % 4, (z + dz + 8) % 8
        return (xx * 2 + yy % 2, zz * 4 + (yy // 2) * 2 + core)

    sibling = (cam, z * 4 + y_hi * 2 + (1 - core))
    mirror = (x * 2 + (1 - y_lo), z * 4 + (1 - y_hi) * 2 + core)
    up, down = device(0, 0, 1), device(0, 0, -1)
    in_plane = [(dx, dy) for dx in range(4) for dy in range(4) if dx + dy > 0]

    my_rows = pl.ds(pl.multiple_of(y_lo * 16, 16), 16)
    my_cols = pl.ds(pl.multiple_of(x * XCOLS, XCOLS), XCOLS)

    loads = [
        pltpu.make_async_copy(k_hbm, kb.at[0, y_hi, core], load_sem.at[0]),
        pltpu.make_async_copy(v_hbm.at[my_rows, my_cols], vb.at[0, y_hi, core, my_rows, my_cols], load_sem.at[1]),
        pltpu.make_async_copy(q_hbm, q, load_sem.at[2]),
        pltpu.make_async_copy(cv_hbm, cv, load_sem.at[3]),
    ]
    for copy in loads:
        copy.start()

    barrier = pltpu.get_barrier_semaphore()
    partners = [sibling] + [device(dx, dy, 0) for dx, dy in in_plane] + [device(0, 0, dz) for dz in range(1, 8)]
    for partner in partners:
        pl.semaphore_signal(barrier, inc=1, device_id=partner, device_id_type=pl.DeviceIdType.MESH)
    pl.semaphore_wait(barrier, len(partners))

    drains = []

    def send(src, dst, send_sem, recv_sem, to):
        copy = pltpu.make_async_remote_copy(
            src_ref=src, dst_ref=dst, send_sem=send_sem, recv_sem=recv_sem,
            device_id=to, device_id_type=pl.DeviceIdType.MESH,
        )
        copy.start()
        return copy

    def half(p):
        return y_hi if p == 0 else 1 - y_hi

    class Ring:
        def __init__(self, buf, send_sem, recv_sem, s_send, s_recv):
            self.buf, self.send_sem, self.recv_sem = buf, send_sem, recv_sem
            self.s_send, self.s_recv = s_send, s_recv

        def block(self, slot, p):
            return self.buf.at[slot, half(p), core]

        def hop(self, slot, p, to, into):
            copy = send(self.block(slot, p), self.block(into, p), self.send_sem.at[into, p], self.recv_sem.at[into, p], to)
            drains.append(copy)

        def share(self, slot, p):
            block = self.block(slot, p)
            drains.append(send(block, block, self.s_send.at[slot, p], self.s_recv.at[slot, p], sibling))

        def near(self):
            block = self.block(0, 0)
            drains.append(send(block, block, self.send_sem.at[0, 0], self.recv_sem.at[0, 1], mirror))
            self.share(0, 0)

        def begin(self, p):
            self.hop(0, p, down, 1)
            self.hop(0, p, up, 2)

        def arrive(self, slot, p):
            block = self.block(slot, p)
            pltpu.make_async_copy(block, block, self.recv_sem.at[slot, p]).wait()
            if slot == 0:
                self.begin(p)
            elif slot in (1, 3) or (slot == 5 and p == 0):
                self.hop(slot, p, down, slot + 2)
            elif slot in (2, 4) or (slot == 6 and p == 1):
                self.hop(slot, p, up, slot + 2 if slot < 6 else 7)
            self.share(slot, p)

        def shared(self, slot):
            for p in range(2):
                block = self.buf.at[slot, half(p), 1 - core]
                pltpu.make_async_copy(block, block, self.s_recv.at[slot, p]).wait()

    keys = Ring(kb, k_send, k_recv, ks_send, ks_recv)

    near, far = pl.ds(0, 4), pl.ds(4, 4)

    def done(ref, sem):
        pltpu.make_async_copy(ref, ref, sem).wait()

    from_z = vb.at[pl.ds(1, 7), y_hi, core, my_rows, my_cols]
    near_piece = vb.at[near, y_hi, core, my_rows, my_cols]
    far_piece = vb.at[far, y_hi, core, my_rows, my_cols]
    near_row = vb.at[near, y_hi, core, my_rows]
    far_column = vb.at[far, :, core, :, my_cols]
    three_pieces = vb.at[near, y_hi, core, my_rows, pl.ds(0, 3 * XCOLS)]
    three_columns = vb.at[far, :, core, :, pl.ds(0, 3 * XCOLS)]

    def values_z():
        piece = vb.at[0, y_hi, core, my_rows, my_cols]
        for s in range(1, SLOTS):
            send(piece, vb.at[s, y_hi, core, my_rows, my_cols], v_send.at[0], v_recv.at[0], device(0, 0, -OFFSETS[s]))

    def values_first():
        done(from_z, v_recv.at[0])
        for d in range(1, 4):
            send(near_piece, near_piece, v_send.at[1], v_recv.at[1], device(d, 0, 0))
            send(far_piece, far_piece, v_send.at[2], v_recv.at[2], device(0, d, 0))

    def values_second():
        done(three_pieces, v_recv.at[1])
        done(three_pieces, v_recv.at[2])
        for d in range(1, 4):
            send(near_row, near_row, v_send.at[6 + d], v_recv.at[3 + d], device(0, d, 0))
            send(far_column, far_column, v_send.at[4], v_recv.at[3], device(d, 0, 0))

    def values_share():
        for d in range(1, 4):
            done(near_row, v_recv.at[3 + d])
        done(three_columns, v_recv.at[3])
        for i, slots in enumerate((near, far)):
            send(vb.at[slots, :, core], vb.at[slots, :, core], v_send.at[5 + i], v_recv.at[7 + i], sibling)

    def values_shared():
        for i, slots in enumerate((near, far)):
            done(vb.at[slots, :, 1 - core], v_recv.at[7 + i])

    def values_sent():
        done(from_z, v_send.at[0])
        done(three_pieces, v_send.at[1])
        done(three_pieces, v_send.at[2])
        for d in range(3):
            done(near_row, v_send.at[7 + d])
        done(three_columns, v_send.at[4])
        for i, slots in enumerate((near, far)):
            done(vb.at[slots, :, core], v_send.at[5 + i])

    def head(h):
        return pl.ds(h * HEAD_DIM if isinstance(h, int) else pl.multiple_of(h * HEAD_DIM, HEAD_DIM), HEAD_DIM)

    def attend(group, first, count):
        slot, ns = GROUPS[group]
        rows = ns * 128

        for h in range(first, first + count):
            key = kb[slot : slot + ns, :, :, :, head(h)].reshape(rows, HEAD_DIM)
            s = lax.dot_general(key, q[:, head(h)], (((1,), (1,)), ((), ())), preferred_element_type=F32)
            u = (jnp.tanh(s * (0.5 / HEAD_DIM**0.5) + bias[h] * 0.5) + 1.0).astype(BF16)
            u_all[h, slot * 128 : slot * 128 + rows, :] = u
            part = jnp.dot(u, cv[:, head(h)], preferred_element_type=F32)
            pb[slot : slot + ns, :, :, :, head(h)] = part.astype(BF16).reshape(ns, 2, 2, ROWS, HEAD_DIM)

    def core_send(group):
        slot, ns = GROUPS[group]
        src = pb.at[pl.ds(slot, ns), :, 1 - core]
        drains.append(send(src, crecv.at[pl.ds(slot, ns)], c_send.at[group], c_recv.at[group], sibling))

    def plane_send(group):
        slot, ns = GROUPS[group]
        block = crecv.at[pl.ds(slot, ns)]
        pltpu.make_async_copy(block, block, c_recv.at[group]).wait()
        for s in range(slot, slot + ns):
            for hi in range(2):
                total = pb[s, hi, core].astype(F32) + crecv[s, hi].astype(F32)
                psend[s, hi] = total.astype(BF16)
        for dx, dy in in_plane:
            xx, yy = (x + dx) % 4, (y + dy) % 4
            rows = pl.ds(pl.multiple_of((yy % 2) * 16, 16), 16)
            cols = pl.ds(pl.multiple_of(xx * XCOLS, XCOLS), XCOLS)
            src = psend.at[pl.ds(slot, ns), yy // 2, rows, cols]
            send(src, precv.at[dx * 4 + dy, pl.ds(slot, ns)], p_send.at[group], p_recv.at[group], device(dx, dy, 0))

    def plane_sum(group):
        slot, ns = GROUPS[group]
        block = precv.at[pl.ds(1, 15), pl.ds(slot, ns)]
        pltpu.make_async_copy(block, block, p_recv.at[group]).wait()
        rows = pl.ds(pl.multiple_of(y_lo * 16, 16), 16)
        cols = pl.ds(pl.multiple_of(x * XCOLS, XCOLS), XCOLS)
        for s in range(slot, slot + ns):
            total = psend[s, y_hi, rows, cols].astype(F32)
            for i in range(1, 16):
                total = total + precv[i, s].astype(F32)
            if s == 0:
                zkeep[...] = total
            else:
                zsend[s] = total.astype(BF16)
                send(zsend.at[s], zrecv.at[s], z_send, z_recv, device(0, 0, OFFSETS[s]))

    def finish():
        block = zrecv.at[pl.ds(1, 7)]
        pltpu.make_async_copy(block, block, z_recv).wait()
        total = zkeep[...]
        for s in range(1, SLOTS):
            total = total + zrecv[s].astype(F32)
        rows = pl.ds(pl.multiple_of(y_lo * 16, 16), 16)
        cols = pl.ds(pl.multiple_of(x * XCOLS, XCOLS), XCOLS)
        lob[rows, cols] = (total * (1.0 / 1024.0)).astype(BF16)
        mine = lob.at[rows, cols]
        for dx in range(4):
            for dl in range(2):
                if dx + dl > 0:
                    to = (((x + dx) % 4) * 2 + (y_lo + dl) % 2, tok)
                    send(mine, mine, l_send, l_recv, to)

    def camera(first, count, unroll):
        def body(i, carry):
            for j in range(unroll):
                h = first + i * unroll + j
                value = vb[:, :, :, :, head(h)].reshape(SLOTS * 128, HEAD_DIM)
                out = jnp.dot(value.T, u_all[h], preferred_element_type=F32)
                co[:, head(h)] = (out * (1.0 / 64.0)).astype(BF16).T
            return carry

        lax.fori_loop(0, count // unroll, body, 0)

    loads[0].wait()
    keys.near()
    keys.begin(0)
    loads[1].wait()
    values_z()
    keys.arrive(0, 1)
    keys.arrive(1, 0)
    keys.arrive(2, 0)
    loads[2].wait()
    loads[3].wait()
    keys.shared(0)
    values_first()
    attend(0, 0, 6)
    keys.arrive(1, 1)
    keys.arrive(2, 1)
    attend(0, 6, 6)
    core_send(0)
    keys.arrive(3, 0)
    keys.arrive(4, 0)
    keys.shared(1)
    keys.shared(2)
    attend(1, 0, 6)
    keys.arrive(3, 1)
    keys.arrive(4, 1)
    values_second()
    plane_send(0)
    attend(1, 6, 6)
    core_send(1)
    keys.arrive(5, 0)
    keys.arrive(6, 0)
    keys.shared(3)
    keys.shared(4)
    attend(2, 0, 6)
    keys.arrive(5, 1)
    keys.arrive(6, 1)
    plane_send(1)
    attend(2, 6, 6)
    core_send(2)
    keys.arrive(7, 0)
    keys.shared(5)
    keys.shared(6)
    attend(3, 0, 6)
    keys.arrive(7, 1)
    plane_send(2)
    plane_sum(0)
    attend(3, 6, 6)
    core_send(3)
    keys.shared(7)
    attend(4, 0, 6)
    plane_send(3)
    plane_sum(1)
    attend(4, 6, 6)
    core_send(4)
    values_share()
    plane_send(4)
    plane_sum(2)
    plane_sum(3)
    values_shared()
    plane_sum(4)
    camera(0, 6, 2)
    finish()
    camera(6, 6, 2)

    block = precv.at[pl.ds(0, 7), 0]
    pltpu.make_async_copy(block, block, l_recv).wait()
    lo[...] = lob[...]
    for copy in drains:
        copy.wait_send()
    values_sent()
    for group, (slot, ns) in enumerate(GROUPS):
        block = precv.at[pl.ds(1, 15), pl.ds(slot, ns)]
        pltpu.make_async_copy(block, block, p_send.at[group]).wait()
    block = zsend.at[pl.ds(1, 7)]
    pltpu.make_async_copy(block, block, z_send).wait()
    block = precv.at[pl.ds(0, 7), 0]
    pltpu.make_async_copy(block, block, l_send).wait()


def shards(camera_q, camera_v, lidar_k, lidar_v, head_bias):
    tokens = camera_q.shape[1]
    hbm = pl.BlockSpec(memory_space=pl.ANY)
    dma = pltpu.SemaphoreType.DMA
    planes = (SLOTS, 2, 2, ROWS, WIDTH)
    camera_out, lidar_out = pl.pallas_call(
        kernel,
        out_shape=[
            pltpu.VMEM((tokens, WIDTH), BF16),
            pltpu.VMEM((ROWS, WIDTH), BF16),
        ],
        in_specs=[hbm, hbm, hbm, hbm, pl.BlockSpec(memory_space=pltpu.SMEM)],
        out_specs=[pl.BlockSpec(memory_space=pltpu.VMEM)] * 2,
        scratch_shapes=[
            pltpu.VMEM((tokens, WIDTH), BF16),
            pltpu.VMEM((tokens, WIDTH), BF16),
            pltpu.VMEM(planes, BF16),
            pltpu.VMEM(planes, BF16),
            pltpu.VMEM((HEADS, SLOTS * 128, tokens), BF16),
            pltpu.VMEM(planes, BF16),
            pltpu.VMEM((SLOTS, 2, ROWS, WIDTH), BF16),
            pltpu.VMEM((SLOTS, 2, ROWS, WIDTH), BF16),
            pltpu.VMEM((16, SLOTS, 16, XCOLS), BF16),
            pltpu.VMEM((16, XCOLS), F32),
            pltpu.VMEM((SLOTS, 16, XCOLS), BF16),
            pltpu.VMEM((SLOTS, 16, XCOLS), BF16),
            pltpu.VMEM((ROWS, WIDTH), BF16),
            dma((4,)),
            dma((SLOTS, 2)), dma((SLOTS, 2)), dma((SLOTS, 2)), dma((SLOTS, 2)),
            dma((10,)), dma((9,)),
            dma((5,)), dma((5,)), dma((5,)), dma((5,)),
            dma, dma, dma, dma,
        ],
        compiler_params=pltpu.CompilerParams(
            collective_id=0, has_side_effects=True, vmem_limit_bytes=54 << 20
        ),
        name="fused",
    )(camera_q.reshape(tokens, WIDTH), camera_v.reshape(tokens, WIDTH), lidar_k, lidar_v, head_bias)
    return camera_out.reshape(camera_q.shape), lidar_out


def solution(mesh):
    return jax.shard_map(
        shards,
        mesh=mesh,
        in_specs=(
            P("cam", "tok", None),
            P("cam", "tok", None),
            P("tok", None),
            P("tok", None),
            P(),
        ),
        out_specs=(P("cam", "tok", None), P("tok", None)),
        check_vma=False,
    )
```

```python
import functools

import jax
import jax.numpy as jnp
from jax import lax
from jax.experimental import pallas as pl
from jax.experimental.pallas import tpu as pltpu
from jax.sharding import PartitionSpec as P

HEADS = 12
HEAD_DIM = 128
WIDTH = HEADS * HEAD_DIM
SLOTS = 8
OFFSETS = (0, 1, -1, 2, -2, 3, -3, 4)
GROUPS = ((0, 1), (1, 2), (3, 2), (5, 2), (7, 1))
ROWS = 32
XCOLS = 384
F32, BF16 = jnp.float32, jnp.bfloat16


def kernel(
    q_hbm, cv_hbm, k_hbm, v_hbm, bias, co, lo,
    q, cv, kb, vb, u_all, pb, crecv, psend, precv, zkeep, zsend, zrecv, lob,
    load_sem, k_send, k_recv, ks_send, ks_recv, v_send, v_recv, w_send, w_recv, ws_send, ws_recv,
    c_send, c_recv, p_send, p_recv, z_send, z_recv, l_send, l_recv,
):
    cam, tok = lax.axis_index("cam"), lax.axis_index("tok")
    x, y_lo = cam // 2, cam % 2
    z, y_hi, core = tok // 4, (tok // 2) % 2, tok % 2
    y = y_hi * 2 + y_lo

    def device(dx, dy, dz):
        xx, yy, zz = (x + dx + 4) % 4, (y + dy + 4) % 4, (z + dz + 8) % 8
        return (xx * 2 + yy % 2, zz * 4 + (yy // 2) * 2 + core)

    sibling = (cam, z * 4 + y_hi * 2 + (1 - core))
    mirror = (x * 2 + (1 - y_lo), z * 4 + (1 - y_hi) * 2 + core)
    up, down = device(0, 0, 1), device(0, 0, -1)
    in_plane = [(dx, dy) for dx in range(4) for dy in range(4) if dx + dy > 0]

    my_rows = pl.ds(pl.multiple_of(y_lo * 16, 16), 16)
    my_cols = pl.ds(pl.multiple_of(x * XCOLS, XCOLS), XCOLS)

    loads = [
        pltpu.make_async_copy(k_hbm, kb.at[0, y_hi, core], load_sem.at[0]),
        pltpu.make_async_copy(v_hbm, vb.at[0, y_hi, core], load_sem.at[1]),
        pltpu.make_async_copy(q_hbm, q, load_sem.at[2]),
        pltpu.make_async_copy(cv_hbm, cv, load_sem.at[3]),
    ]
    for copy in loads:
        copy.start()

    barrier = pltpu.get_barrier_semaphore()
    partners = [sibling] + [device(dx, dy, 0) for dx, dy in in_plane] + [device(0, 0, dz) for dz in range(1, 8)]
    for partner in partners:
        pl.semaphore_signal(barrier, inc=1, device_id=partner, device_id_type=pl.DeviceIdType.MESH)
    pl.semaphore_wait(barrier, len(partners))

    drains = []

    def send(src, dst, send_sem, recv_sem, to):
        copy = pltpu.make_async_remote_copy(
            src_ref=src, dst_ref=dst, send_sem=send_sem, recv_sem=recv_sem,
            device_id=to, device_id_type=pl.DeviceIdType.MESH,
        )
        copy.start()
        return copy

    def half(p):
        return y_hi if p == 0 else 1 - y_hi

    class Ring:
        def __init__(self, buf, send_sem, recv_sem, s_send, s_recv, onward):
            self.onward = onward
            self.buf, self.send_sem, self.recv_sem = buf, send_sem, recv_sem
            self.s_send, self.s_recv = s_send, s_recv

        def block(self, slot, p):
            return self.buf.at[slot, half(p), core]

        def hop(self, slot, p, to, into):
            copy = send(self.block(slot, p), self.block(into, p), self.send_sem.at[into, p], self.recv_sem.at[into, p], to)
            drains.append(copy)

        def share(self, slot, p):
            block = self.block(slot, p)
            drains.append(send(block, block, self.s_send.at[slot, p], self.s_recv.at[slot, p], sibling))

        def near(self):
            block = self.block(0, 0)
            drains.append(send(block, block, self.send_sem.at[0, 0], self.recv_sem.at[0, 1], mirror))
            self.share(0, 0)

        def begin(self, p):
            self.hop(0, p, down, 1)
            self.hop(0, p, up, 2)

        def arrive(self, slot, p):
            block = self.block(slot, p)
            pltpu.make_async_copy(block, block, self.recv_sem.at[slot, p]).wait()
            if slot == 0:
                self.begin(p)
            elif not self.onward:
                pass
            elif slot in (1, 3) or (slot == 5 and p == 0):
                self.hop(slot, p, down, slot + 2)
            elif slot in (2, 4) or (slot == 6 and p == 1):
                self.hop(slot, p, up, slot + 2 if slot < 6 else 7)
            self.share(slot, p)

        def shared(self, slot):
            for p in range(2):
                block = self.buf.at[slot, half(p), 1 - core]
                pltpu.make_async_copy(block, block, self.s_recv.at[slot, p]).wait()

    keys = Ring(kb, k_send, k_recv, ks_send, ks_recv, True)
    values = Ring(vb, w_send, w_recv, ws_send, ws_recv, False)

    near, far = pl.ds(3, 2), pl.ds(5, 3)

    def done(ref, sem):
        pltpu.make_async_copy(ref, ref, sem).wait()

    from_z = vb.at[pl.ds(3, 5), y_hi, core, my_rows, my_cols]
    near_piece = vb.at[near, y_hi, core, my_rows, my_cols]
    far_piece = vb.at[far, y_hi, core, my_rows, my_cols]
    near_row = vb.at[near, y_hi, core, my_rows]
    far_column = vb.at[far, :, core, :, my_cols]
    three_near = vb.at[near, y_hi, core, my_rows, pl.ds(0, 3 * XCOLS)]
    three_far = vb.at[far, y_hi, core, my_rows, pl.ds(0, 3 * XCOLS)]
    three_columns = vb.at[far, :, core, :, pl.ds(0, 3 * XCOLS)]

    def values_z():
        piece = vb.at[0, y_hi, core, my_rows, my_cols]
        for s in range(3, SLOTS):
            send(piece, vb.at[s, y_hi, core, my_rows, my_cols], v_send.at[0], v_recv.at[0], device(0, 0, -OFFSETS[s]))

    def values_first():
        done(from_z, v_recv.at[0])
        for d in range(1, 4):
            send(near_piece, near_piece, v_send.at[1], v_recv.at[1], device(d, 0, 0))
            send(far_piece, far_piece, v_send.at[2], v_recv.at[2], device(0, d, 0))

    def values_second():
        done(three_near, v_recv.at[1])
        done(three_far, v_recv.at[2])
        for d in range(1, 4):
            send(near_row, near_row, v_send.at[6 + d], v_recv.at[3 + d], device(0, d, 0))
            send(far_column, far_column, v_send.at[4], v_recv.at[3], device(d, 0, 0))

    def values_share():
        for d in range(1, 4):
            done(near_row, v_recv.at[3 + d])
        done(three_columns, v_recv.at[3])
        for i, slots in enumerate((near, far)):
            send(vb.at[slots, :, core], vb.at[slots, :, core], v_send.at[5 + i], v_recv.at[7 + i], sibling)

    def values_shared():
        for i, slots in enumerate((near, far)):
            done(vb.at[slots, :, 1 - core], v_recv.at[7 + i])

    def values_sent():
        done(from_z, v_send.at[0])
        done(three_near, v_send.at[1])
        done(three_far, v_send.at[2])
        for d in range(3):
            done(near_row, v_send.at[7 + d])
        done(three_columns, v_send.at[4])
        for i, slots in enumerate((near, far)):
            done(vb.at[slots, :, core], v_send.at[5 + i])

    def head(h):
        return pl.ds(h * HEAD_DIM if isinstance(h, int) else pl.multiple_of(h * HEAD_DIM, HEAD_DIM), HEAD_DIM)

    def attend(group, first, count):
        slot, ns = GROUPS[group]
        rows = ns * 128

        for h in range(first, first + count):
            key = kb[slot : slot + ns, :, :, :, head(h)].reshape(rows, HEAD_DIM)
            s = lax.dot_general(key, q[:, head(h)], (((1,), (1,)), ((), ())), preferred_element_type=F32)
            u = (jnp.tanh(s * (0.5 / HEAD_DIM**0.5) + bias[h] * 0.5) + 1.0).astype(BF16)
            u_all[h, slot * 128 : slot * 128 + rows, :] = u
            part = jnp.dot(u, cv[:, head(h)], preferred_element_type=F32)
            pb[slot : slot + ns, :, :, :, head(h)] = part.astype(BF16).reshape(ns, 2, 2, ROWS, HEAD_DIM)

    def core_send(group):
        slot, ns = GROUPS[group]
        src = pb.at[pl.ds(slot, ns), :, 1 - core]
        drains.append(send(src, crecv.at[pl.ds(slot, ns)], c_send.at[group], c_recv.at[group], sibling))

    def plane_send(group):
        slot, ns = GROUPS[group]
        block = crecv.at[pl.ds(slot, ns)]
        pltpu.make_async_copy(block, block, c_recv.at[group]).wait()
        for s in range(slot, slot + ns):
            for hi in range(2):
                total = pb[s, hi, core].astype(F32) + crecv[s, hi].astype(F32)
                psend[s, hi] = total.astype(BF16)
        for dx, dy in in_plane:
            xx, yy = (x + dx) % 4, (y + dy) % 4
            rows = pl.ds(pl.multiple_of((yy % 2) * 16, 16), 16)
            cols = pl.ds(pl.multiple_of(xx * XCOLS, XCOLS), XCOLS)
            src = psend.at[pl.ds(slot, ns), yy // 2, rows, cols]
            send(src, precv.at[dx * 4 + dy, pl.ds(slot, ns)], p_send.at[group], p_recv.at[group], device(dx, dy, 0))

    def plane_sum(group):
        slot, ns = GROUPS[group]
        block = precv.at[pl.ds(1, 15), pl.ds(slot, ns)]
        pltpu.make_async_copy(block, block, p_recv.at[group]).wait()
        rows = pl.ds(pl.multiple_of(y_lo * 16, 16), 16)
        cols = pl.ds(pl.multiple_of(x * XCOLS, XCOLS), XCOLS)
        for s in range(slot, slot + ns):
            total = psend[s, y_hi, rows, cols].astype(F32)
            for i in range(1, 16):
                total = total + precv[i, s].astype(F32)
            if s == 0:
                zkeep[...] = total
            else:
                zsend[s] = total.astype(BF16)
                send(zsend.at[s], zrecv.at[s], z_send, z_recv, device(0, 0, OFFSETS[s]))

    def finish():
        block = zrecv.at[pl.ds(1, 7)]
        pltpu.make_async_copy(block, block, z_recv).wait()
        total = zkeep[...]
        for s in range(1, SLOTS):
            total = total + zrecv[s].astype(F32)
        rows = pl.ds(pl.multiple_of(y_lo * 16, 16), 16)
        cols = pl.ds(pl.multiple_of(x * XCOLS, XCOLS), XCOLS)
        lob[rows, cols] = (total * (1.0 / 1024.0)).astype(BF16)
        mine = lob.at[rows, cols]
        for dx in range(4):
            for dl in range(2):
                if dx + dl > 0:
                    to = (((x + dx) % 4) * 2 + (y_lo + dl) % 2, tok)
                    send(mine, mine, l_send, l_recv, to)

    def camera(first, count, unroll):
        def body(i, carry):
            for j in range(unroll):
                h = first + i * unroll + j
                value = vb[:, :, :, :, head(h)].reshape(SLOTS * 128, HEAD_DIM)
                out = jnp.dot(value.T, u_all[h], preferred_element_type=F32)
                co[:, head(h)] = (out * (1.0 / 64.0)).astype(BF16).T
            return carry

        lax.fori_loop(0, count // unroll, body, 0)

    loads[0].wait()
    keys.near()
    keys.begin(0)
    loads[1].wait()
    values_z()
    keys.arrive(0, 1)
    values.near()
    keys.arrive(1, 0)
    keys.arrive(2, 0)
    loads[2].wait()
    loads[3].wait()
    keys.shared(0)
    values_first()
    attend(0, 0, 6)
    keys.arrive(1, 1)
    keys.arrive(2, 1)
    attend(0, 6, 6)
    core_send(0)
    keys.arrive(3, 0)
    keys.arrive(4, 0)
    keys.shared(1)
    keys.shared(2)
    attend(1, 0, 6)
    keys.arrive(3, 1)
    keys.arrive(4, 1)
    values_second()
    plane_send(0)
    attend(1, 6, 6)
    core_send(1)
    keys.arrive(5, 0)
    keys.arrive(6, 0)
    keys.shared(3)
    keys.shared(4)
    attend(2, 0, 6)
    keys.arrive(5, 1)
    keys.arrive(6, 1)
    values.begin(0)
    values.arrive(0, 1)
    plane_send(1)
    attend(2, 6, 6)
    core_send(2)
    keys.arrive(7, 0)
    keys.shared(5)
    keys.shared(6)
    attend(3, 0, 6)
    keys.arrive(7, 1)
    plane_send(2)
    plane_sum(0)
    attend(3, 6, 6)
    core_send(3)
    keys.shared(7)
    attend(4, 0, 6)
    plane_send(3)
    plane_sum(1)
    attend(4, 6, 6)
    core_send(4)
    for s in range(1, 3):
        for p in range(2):
            values.arrive(s, p)
    plane_sum(2)
    plane_send(4)
    values_share()
    plane_sum(3)
    plane_sum(4)
    for s in range(3):
        values.shared(s)
    values_shared()
    camera(0, 6, 2)
    finish()
    camera(6, 6, 2)

    block = precv.at[pl.ds(0, 7), 0]
    pltpu.make_async_copy(block, block, l_recv).wait()
    lo[...] = lob[...]
    for copy in drains:
        copy.wait_send()
    values_sent()
    for group, (slot, ns) in enumerate(GROUPS):
        block = precv.at[pl.ds(1, 15), pl.ds(slot, ns)]
        pltpu.make_async_copy(block, block, p_send.at[group]).wait()
    block = zsend.at[pl.ds(1, 7)]
    pltpu.make_async_copy(block, block, z_send).wait()
    block = precv.at[pl.ds(0, 7), 0]
    pltpu.make_async_copy(block, block, l_send).wait()


def shards(camera_q, camera_v, lidar_k, lidar_v, head_bias):
    tokens = camera_q.shape[1]
    hbm = pl.BlockSpec(memory_space=pl.ANY)
    dma = pltpu.SemaphoreType.DMA
    planes = (SLOTS, 2, 2, ROWS, WIDTH)
    camera_out, lidar_out = pl.pallas_call(
        kernel,
        out_shape=[
            pltpu.VMEM((tokens, WIDTH), BF16),
            pltpu.VMEM((ROWS, WIDTH), BF16),
        ],
        in_specs=[hbm, hbm, hbm, hbm, pl.BlockSpec(memory_space=pltpu.SMEM)],
        out_specs=[pl.BlockSpec(memory_space=pltpu.VMEM)] * 2,
        scratch_shapes=[
            pltpu.VMEM((tokens, WIDTH), BF16),
            pltpu.VMEM((tokens, WIDTH), BF16),
            pltpu.VMEM(planes, BF16),
            pltpu.VMEM(planes, BF16),
            pltpu.VMEM((HEADS, SLOTS * 128, tokens), BF16),
            pltpu.VMEM(planes, BF16),
            pltpu.VMEM((SLOTS, 2, ROWS, WIDTH), BF16),
            pltpu.VMEM((SLOTS, 2, ROWS, WIDTH), BF16),
            pltpu.VMEM((16, SLOTS, 16, XCOLS), BF16),
            pltpu.VMEM((16, XCOLS), F32),
            pltpu.VMEM((SLOTS, 16, XCOLS), BF16),
            pltpu.VMEM((SLOTS, 16, XCOLS), BF16),
            pltpu.VMEM((ROWS, WIDTH), BF16),
            dma((4,)),
            dma((SLOTS, 2)), dma((SLOTS, 2)), dma((SLOTS, 2)), dma((SLOTS, 2)),
            dma((10,)), dma((9,)),
            dma((3, 2)), dma((3, 2)), dma((3, 2)), dma((3, 2)),
            dma((5,)), dma((5,)), dma((5,)), dma((5,)),
            dma, dma, dma, dma,
        ],
        compiler_params=pltpu.CompilerParams(
            collective_id=0, has_side_effects=True, vmem_limit_bytes=54 << 20
        ),
        name="fused",
    )(camera_q.reshape(tokens, WIDTH), camera_v.reshape(tokens, WIDTH), lidar_k, lidar_v, head_bias)
    return camera_out.reshape(camera_q.shape), lidar_out


def solution(mesh):
    return jax.shard_map(
        shards,
        mesh=mesh,
        in_specs=(
            P("cam", "tok", None),
            P("cam", "tok", None),
            P("tok", None),
            P("tok", None),
            P(),
        ),
        out_specs=(P("cam", "tok", None), P("tok", None)),
        check_vma=False,
    )
```

```python
import functools

import jax
import jax.numpy as jnp
from jax import lax
from jax.experimental import pallas as pl
from jax.experimental.pallas import tpu as pltpu
from jax.sharding import PartitionSpec as P

HEADS = 12
HEAD_DIM = 128
WIDTH = HEADS * HEAD_DIM
SLOTS = 8
OFFSETS = (0, 1, -1, 2, -2, 3, -3, 4)
GROUPS = ((0, 1), (1, 2), (3, 2), (5, 2), (7, 1))
ROWS = 32
XCOLS = 384
F32, BF16 = jnp.float32, jnp.bfloat16


def kernel(
    q_hbm, cv_hbm, k_hbm, v_hbm, bias, co, lo,
    q, cv, kb, vb, u_all, pb, crecv, psend, precv, zkeep, zsend, zrecv, lob,
    load_sem, k_send, k_recv, ks_send, ks_recv, v_send, v_recv, w_send, w_recv, ws_send, ws_recv,
    c_send, c_recv, p_send, p_recv, z_send, z_recv, l_send, l_recv,
):
    cam, tok = lax.axis_index("cam"), lax.axis_index("tok")
    x, y_lo = cam // 2, cam % 2
    z, y_hi, core = tok // 4, (tok // 2) % 2, tok % 2
    y = y_hi * 2 + y_lo

    def device(dx, dy, dz):
        xx, yy, zz = (x + dx + 4) % 4, (y + dy + 4) % 4, (z + dz + 8) % 8
        return (xx * 2 + yy % 2, zz * 4 + (yy // 2) * 2 + core)

    sibling = (cam, z * 4 + y_hi * 2 + (1 - core))
    mirror = (x * 2 + (1 - y_lo), z * 4 + (1 - y_hi) * 2 + core)
    up, down = device(0, 0, 1), device(0, 0, -1)
    in_plane = [(dx, dy) for dx in range(4) for dy in range(4) if dx + dy > 0]

    my_rows = pl.ds(pl.multiple_of(y_lo * 16, 16), 16)
    my_cols = pl.ds(pl.multiple_of(x * XCOLS, XCOLS), XCOLS)

    loads = [
        pltpu.make_async_copy(k_hbm, kb.at[0, y_hi, core], load_sem.at[0]),
        pltpu.make_async_copy(v_hbm, vb.at[0, y_hi, core], load_sem.at[1]),
        pltpu.make_async_copy(q_hbm, q, load_sem.at[2]),
        pltpu.make_async_copy(cv_hbm, cv, load_sem.at[3]),
    ]
    for copy in loads:
        copy.start()

    barrier = pltpu.get_barrier_semaphore()
    partners = [sibling] + [device(dx, dy, 0) for dx, dy in in_plane] + [device(0, 0, dz) for dz in range(1, 8)]
    for partner in partners:
        pl.semaphore_signal(barrier, inc=1, device_id=partner, device_id_type=pl.DeviceIdType.MESH)
    pl.semaphore_wait(barrier, len(partners))

    drains = []

    def send(src, dst, send_sem, recv_sem, to):
        copy = pltpu.make_async_remote_copy(
            src_ref=src, dst_ref=dst, send_sem=send_sem, recv_sem=recv_sem,
            device_id=to, device_id_type=pl.DeviceIdType.MESH,
        )
        copy.start()
        return copy

    def half(p):
        return y_hi if p == 0 else 1 - y_hi

    class Ring:
        def __init__(self, buf, send_sem, recv_sem, s_send, s_recv, onward):
            self.onward = onward
            self.buf, self.send_sem, self.recv_sem = buf, send_sem, recv_sem
            self.s_send, self.s_recv = s_send, s_recv

        def block(self, slot, p):
            return self.buf.at[slot, half(p), core]

        def hop(self, slot, p, to, into):
            copy = send(self.block(slot, p), self.block(into, p), self.send_sem.at[into, p], self.recv_sem.at[into, p], to)
            drains.append(copy)

        def share(self, slot, p):
            block = self.block(slot, p)
            drains.append(send(block, block, self.s_send.at[slot, p], self.s_recv.at[slot, p], sibling))

        def near(self):
            block = self.block(0, 0)
            drains.append(send(block, block, self.send_sem.at[0, 0], self.recv_sem.at[0, 1], mirror))
            self.share(0, 0)

        def begin(self, p):
            self.hop(0, p, down, 1)
            self.hop(0, p, up, 2)

        def arrive(self, slot, p):
            block = self.block(slot, p)
            pltpu.make_async_copy(block, block, self.recv_sem.at[slot, p]).wait()
            if slot == 0:
                self.begin(p)
            elif not self.onward:
                pass
            elif slot in (1, 3) or (slot == 5 and p == 0):
                self.hop(slot, p, down, slot + 2)
            elif slot in (2, 4) or (slot == 6 and p == 1):
                self.hop(slot, p, up, slot + 2 if slot < 6 else 7)
            self.share(slot, p)

        def shared(self, slot):
            for p in range(2):
                block = self.buf.at[slot, half(p), 1 - core]
                pltpu.make_async_copy(block, block, self.s_recv.at[slot, p]).wait()

    keys = Ring(kb, k_send, k_recv, ks_send, ks_recv, True)
    values = Ring(vb, w_send, w_recv, ws_send, ws_recv, False)

    near, far = pl.ds(3, 2), pl.ds(5, 3)

    def done(ref, sem):
        pltpu.make_async_copy(ref, ref, sem).wait()

    from_z = vb.at[pl.ds(3, 5), y_hi, core, my_rows, my_cols]
    near_piece = vb.at[near, y_hi, core, my_rows, my_cols]
    far_piece = vb.at[far, y_hi, core, my_rows, my_cols]
    near_row = vb.at[near, y_hi, core, my_rows]
    far_column = vb.at[far, :, core, :, my_cols]
    three_near = vb.at[near, y_hi, core, my_rows, pl.ds(0, 3 * XCOLS)]
    three_far = vb.at[far, y_hi, core, my_rows, pl.ds(0, 3 * XCOLS)]
    three_columns = vb.at[far, :, core, :, pl.ds(0, 3 * XCOLS)]

    def values_z():
        piece = vb.at[0, y_hi, core, my_rows, my_cols]
        for s in range(3, SLOTS):
            send(piece, vb.at[s, y_hi, core, my_rows, my_cols], v_send.at[0], v_recv.at[0], device(0, 0, -OFFSETS[s]))

    def values_first():
        done(from_z, v_recv.at[0])
        for d in range(1, 4):
            send(near_piece, near_piece, v_send.at[1], v_recv.at[1], device(d, 0, 0))
            send(far_piece, far_piece, v_send.at[2], v_recv.at[2], device(0, d, 0))

    def values_second():
        done(three_near, v_recv.at[1])
        done(three_far, v_recv.at[2])
        for d in range(1, 4):
            send(near_row, near_row, v_send.at[6 + d], v_recv.at[3 + d], device(0, d, 0))
            send(far_column, far_column, v_send.at[4], v_recv.at[3], device(d, 0, 0))

    def values_share():
        for d in range(1, 4):
            done(near_row, v_recv.at[3 + d])
        done(three_columns, v_recv.at[3])
        for i, slots in enumerate((near, far)):
            send(vb.at[slots, :, core], vb.at[slots, :, core], v_send.at[5 + i], v_recv.at[7 + i], sibling)

    def values_shared():
        for i, slots in enumerate((near, far)):
            done(vb.at[slots, :, 1 - core], v_recv.at[7 + i])

    def values_sent():
        done(from_z, v_send.at[0])
        done(three_near, v_send.at[1])
        done(three_far, v_send.at[2])
        for d in range(3):
            done(near_row, v_send.at[7 + d])
        done(three_columns, v_send.at[4])
        for i, slots in enumerate((near, far)):
            done(vb.at[slots, :, core], v_send.at[5 + i])

    def head(h):
        return pl.ds(h * HEAD_DIM if isinstance(h, int) else pl.multiple_of(h * HEAD_DIM, HEAD_DIM), HEAD_DIM)

    def attend(group, first, count):
        slot, ns = GROUPS[group]
        rows = ns * 128

        for h in range(first, first + count):
            key = kb[slot : slot + ns, :, :, :, head(h)].reshape(rows, HEAD_DIM)
            s = lax.dot_general(key, q[:, head(h)], (((1,), (1,)), ((), ())), preferred_element_type=F32)
            u = (jnp.tanh(s * (0.5 / HEAD_DIM**0.5) + bias[h] * 0.5) + 1.0).astype(BF16)
            u_all[h, slot * 128 : slot * 128 + rows, :] = u
            part = jnp.dot(u, cv[:, head(h)], preferred_element_type=F32)
            pb[slot : slot + ns, :, :, :, head(h)] = part.astype(BF16).reshape(ns, 2, 2, ROWS, HEAD_DIM)

    def core_send(group):
        slot, ns = GROUPS[group]
        src = pb.at[pl.ds(slot, ns), :, 1 - core]
        drains.append(send(src, crecv.at[pl.ds(slot, ns)], c_send.at[group], c_recv.at[group], sibling))

    def plane_send(group):
        slot, ns = GROUPS[group]
        block = crecv.at[pl.ds(slot, ns)]
        pltpu.make_async_copy(block, block, c_recv.at[group]).wait()
        for s in range(slot, slot + ns):
            for hi in range(2):
                total = pb[s, hi, core].astype(F32) + crecv[s, hi].astype(F32)
                psend[s, hi] = total.astype(BF16)
        for dx, dy in in_plane:
            xx, yy = (x + dx) % 4, (y + dy) % 4
            rows = pl.ds(pl.multiple_of((yy % 2) * 16, 16), 16)
            cols = pl.ds(pl.multiple_of(xx * XCOLS, XCOLS), XCOLS)
            src = psend.at[pl.ds(slot, ns), yy // 2, rows, cols]
            send(src, precv.at[dx * 4 + dy, pl.ds(slot, ns)], p_send.at[group], p_recv.at[group], device(dx, dy, 0))

    def plane_sum(group):
        slot, ns = GROUPS[group]
        block = precv.at[pl.ds(1, 15), pl.ds(slot, ns)]
        pltpu.make_async_copy(block, block, p_recv.at[group]).wait()
        rows = pl.ds(pl.multiple_of(y_lo * 16, 16), 16)
        cols = pl.ds(pl.multiple_of(x * XCOLS, XCOLS), XCOLS)
        for s in range(slot, slot + ns):
            total = psend[s, y_hi, rows, cols].astype(F32)
            for i in range(1, 16):
                total = total + precv[i, s].astype(F32)
            if s == 0:
                zkeep[...] = total
            else:
                zsend[s] = total.astype(BF16)
                send(zsend.at[s], zrecv.at[s], z_send, z_recv, device(0, 0, OFFSETS[s]))

    def finish():
        block = zrecv.at[pl.ds(1, 7)]
        pltpu.make_async_copy(block, block, z_recv).wait()
        total = zkeep[...]
        for s in range(1, SLOTS):
            total = total + zrecv[s].astype(F32)
        rows = pl.ds(pl.multiple_of(y_lo * 16, 16), 16)
        cols = pl.ds(pl.multiple_of(x * XCOLS, XCOLS), XCOLS)
        lob[rows, cols] = (total * (1.0 / 1024.0)).astype(BF16)
        mine = lob.at[rows, cols]
        for dx in range(4):
            for dl in range(2):
                if dx + dl > 0:
                    to = (((x + dx) % 4) * 2 + (y_lo + dl) % 2, tok)
                    send(mine, mine, l_send, l_recv, to)

    def camera(first, count, unroll):
        def body(i, carry):
            for j in range(unroll):
                h = first + i * unroll + j
                value = vb[:, :, :, :, head(h)].reshape(SLOTS * 128, HEAD_DIM)
                out = jnp.dot(value.T, u_all[h], preferred_element_type=F32)
                co[:, head(h)] = (out * (1.0 / 64.0)).astype(BF16).T
            return carry

        lax.fori_loop(0, count // unroll, body, 0)

    loads[0].wait()
    keys.near()
    keys.begin(0)
    loads[1].wait()
    values_z()
    keys.arrive(0, 1)
    values.near()
    keys.arrive(1, 0)
    keys.arrive(2, 0)
    loads[2].wait()
    loads[3].wait()
    keys.shared(0)
    values_first()
    attend(0, 0, 6)
    keys.arrive(1, 1)
    keys.arrive(2, 1)
    attend(0, 6, 6)
    core_send(0)
    keys.arrive(3, 0)
    keys.arrive(4, 0)
    keys.shared(1)
    keys.shared(2)
    attend(1, 0, 6)
    keys.arrive(3, 1)
    keys.arrive(4, 1)
    values_second()
    plane_send(0)
    attend(1, 6, 6)
    core_send(1)
    keys.arrive(5, 0)
    keys.arrive(6, 0)
    keys.shared(3)
    keys.shared(4)
    attend(2, 0, 6)
    keys.arrive(5, 1)
    keys.arrive(6, 1)
    values.begin(0)
    values.arrive(0, 1)
    plane_send(1)
    attend(2, 6, 6)
    core_send(2)
    keys.arrive(7, 0)
    keys.shared(5)
    keys.shared(6)
    attend(3, 0, 6)
    keys.arrive(7, 1)
    plane_send(2)
    plane_sum(0)
    attend(3, 6, 6)
    core_send(3)
    keys.shared(7)
    attend(4, 0, 6)
    plane_send(3)
    plane_sum(1)
    attend(4, 6, 6)
    core_send(4)
    plane_send(4)
    for s in range(1, 3):
        for p in range(2):
            values.arrive(s, p)
    plane_sum(2)
    values_share()
    plane_sum(3)
    plane_sum(4)
    for s in range(3):
        values.shared(s)
    values_shared()
    camera(0, 6, 2)
    finish()
    camera(6, 6, 2)

    block = precv.at[pl.ds(0, 7), 0]
    pltpu.make_async_copy(block, block, l_recv).wait()
    lo[...] = lob[...]
    for copy in drains:
        copy.wait_send()
    values_sent()
    for group, (slot, ns) in enumerate(GROUPS):
        block = precv.at[pl.ds(1, 15), pl.ds(slot, ns)]
        pltpu.make_async_copy(block, block, p_send.at[group]).wait()
    block = zsend.at[pl.ds(1, 7)]
    pltpu.make_async_copy(block, block, z_send).wait()
    block = precv.at[pl.ds(0, 7), 0]
    pltpu.make_async_copy(block, block, l_send).wait()


def shards(camera_q, camera_v, lidar_k, lidar_v, head_bias):
    tokens = camera_q.shape[1]
    hbm = pl.BlockSpec(memory_space=pl.ANY)
    dma = pltpu.SemaphoreType.DMA
    planes = (SLOTS, 2, 2, ROWS, WIDTH)
    camera_out, lidar_out = pl.pallas_call(
        kernel,
        out_shape=[
            pltpu.VMEM((tokens, WIDTH), BF16),
            pltpu.VMEM((ROWS, WIDTH), BF16),
        ],
        in_specs=[hbm, hbm, hbm, hbm, pl.BlockSpec(memory_space=pltpu.SMEM)],
        out_specs=[pl.BlockSpec(memory_space=pltpu.VMEM)] * 2,
        scratch_shapes=[
            pltpu.VMEM((tokens, WIDTH), BF16),
            pltpu.VMEM((tokens, WIDTH), BF16),
            pltpu.VMEM(planes, BF16),
            pltpu.VMEM(planes, BF16),
            pltpu.VMEM((HEADS, SLOTS * 128, tokens), BF16),
            pltpu.VMEM(planes, BF16),
            pltpu.VMEM((SLOTS, 2, ROWS, WIDTH), BF16),
            pltpu.VMEM((SLOTS, 2, ROWS, WIDTH), BF16),
            pltpu.VMEM((16, SLOTS, 16, XCOLS), BF16),
            pltpu.VMEM((16, XCOLS), F32),
            pltpu.VMEM((SLOTS, 16, XCOLS), BF16),
            pltpu.VMEM((SLOTS, 16, XCOLS), BF16),
            pltpu.VMEM((ROWS, WIDTH), BF16),
            dma((4,)),
            dma((SLOTS, 2)), dma((SLOTS, 2)), dma((SLOTS, 2)), dma((SLOTS, 2)),
            dma((10,)), dma((9,)),
            dma((3, 2)), dma((3, 2)), dma((3, 2)), dma((3, 2)),
            dma((5,)), dma((5,)), dma((5,)), dma((5,)),
            dma, dma, dma, dma,
        ],
        compiler_params=pltpu.CompilerParams(
            collective_id=0, has_side_effects=True, vmem_limit_bytes=54 << 20
        ),
        name="fused",
    )(camera_q.reshape(tokens, WIDTH), camera_v.reshape(tokens, WIDTH), lidar_k, lidar_v, head_bias)
    return camera_out.reshape(camera_q.shape), lidar_out


def solution(mesh):
    return jax.shard_map(
        shards,
        mesh=mesh,
        in_specs=(
            P("cam", "tok", None),
            P("cam", "tok", None),
            P("tok", None),
            P("tok", None),
            P(),
        ),
        out_specs=(P("cam", "tok", None), P("tok", None)),
        check_vma=False,
    )
```
